32 devices in a mesh: groups: 2 (over y), trace: 4 (over z), space: 2 (over x), sub: 2 (over core).
Axes of the slice: x: 2, y: 2, z: 4, core: 2. Of those that a mesh axis runs over, the one named last changes fastest.
Arguments:
- seismic: bfloat16 [256, 1024, 128], P(('groups', 'trace', 'space', 'sub')), parts along dimension 0, may hold values from -6 to 6
- band_low: int32 [256], P('groups'), parts along dimension 0, may hold values from 0 to 127
- band_high: int32 [256], P('groups'), parts along dimension 0, may hold values from 256 to 512
- leaf_weights: bfloat16 [8, 512, 2, 64], replicated, may hold values from -0.15625 to 0.15625
- translations: float32 [32, 2, 64, 64], replicated, may hold values from -1 to 1
- level_table: int32 [3, 8, 2], replicated, may hold values from 0 to 31
Outputs:
- image_weights: float32 [16, 2, 64, 128], P(('groups', 'trace', 'space'), None, 'sub'), parts along dimension 0
The draws below stay inside these ranges and needn't reach their ends.
There are 2 independent parts, one for each index of `groups`. The reference program is written for one: setup_inputs(seed, part) draws one part's arguments, and reference() takes and returns one part's arrays. A program takes and returns all parts, laid end to end along the dimension named above; an argument that names none is the same for every part. Nothing has to cross between parts.
All inputs are finite; a program needn't handle non-finite values.
Results may differ from the reference program's by a relative error of at most 0.0037.
Values may be sent and summed in bfloat16 or wider, within the bound.
A program may use at most 64 MiB of HBM per device.

```python
import math
import jax
import jax.numpy as jnp
from jax import lax

SHOTS = 128
TR_DEV = 8
NT = 1024
F = 512
R = 64
NMAT = 32
TRACES = 128
NBOX = 8
SPACE_BITS = 1
TRACE_BITS = 2
LEVEL_ROWS = 3
N_TRACE = 4
N_SPACE = 2
N_SUB = 2


def set_ends(array, key, smallest, high):
    longest = array.shape.index(max(array.shape))
    spots = []
    for shift in (0, 1):
        where = [jax.random.randint(jax.random.fold_in(key, axis), (), 0, length) for axis, length in enumerate(array.shape)]
        where[longest] = (where[longest] + shift) % array.shape[longest]
        spots.append(tuple(where))
    return array.at[spots[0]].set(smallest).at[spots[1]].set(high)


def steps_of(own_key, extent, split, low, high):
    loudness = 1.0
    for dim, blocks in split:
        draws = jax.random.uniform(jax.random.fold_in(jax.random.fold_in(own_key, 6), dim), (blocks,), jnp.float32, low / len(split), high / len(split))
        loudness = loudness * jnp.repeat(jnp.exp(draws), extent[dim] // blocks).reshape((-1,) + (1,) * (len(extent) - 1 - dim))
    return loudness


def gaussian(stream_key, shape, scale, reach, split=(), held_as=jnp.bfloat16):
    values = scale * jax.random.normal(stream_key, shape, jnp.float32)
    if split:
        values = values * steps_of(stream_key, shape, split, -0.22, 0.18)
    return jnp.clip(values, -reach, reach).astype(held_as)


def setup_inputs(seed: int = 0, part: int = 0) -> dict:
    key_of = jax.random.split(jax.random.key(seed), 7)
    part_splits = jax.random.split(jax.random.fold_in(key_of[6], part), 7)
    return {
        "seismic": gaussian(part_splits[0], (TRACES, NT, SHOTS), 1.0, 6.0, ((0, 16),)),
        "band_low": set_ends(jax.random.randint(part_splits[1], (SHOTS,), 0, F // 4), jax.random.fold_in(part_splits[1], 1), 0, (F // 4) - 1).astype(jnp.int32),
        "band_high": set_ends(jax.random.randint(part_splits[2], (SHOTS,), F // 2, F + 1), jax.random.fold_in(part_splits[2], 1), F // 2, F).astype(jnp.int32),
        "leaf_weights": gaussian(key_of[3], (TR_DEV, F, 2, R), (1.0 / (TR_DEV * N_TRACE * N_SUB * (F // N_TRACE)) ** 0.5), 0.15625),
        "translations": gaussian(key_of[4], (NMAT, 2, R, R), (0.5 / R ** 0.5), 1.0, (), jnp.float32),
        "level_table": set_ends(jax.random.randint(key_of[5], (LEVEL_ROWS, NBOX, 2), 0, NMAT), jax.random.fold_in(key_of[5], 1), 0, NMAT - 1).astype(jnp.int32),
    }


def spectral_table(freq_total, samples):
    freq_range = jnp.arange(freq_total, dtype=jnp.int32)
    time_range = jnp.arange(samples, dtype=jnp.int32)
    phase = freq_range[:, None] * time_range[None, :] % samples
    angle = phase.astype(jnp.float32) * (2.0 * math.pi / samples)
    factor = 1.0 / math.sqrt(samples)
    return (jnp.concatenate([jnp.cos(angle), -jnp.sin(angle)], axis=0) * factor).astype(jnp.bfloat16)

def complex_product(left, right):
    highest = lax.Precision.HIGHEST
    real_part = jnp.dot(left[0], right[0], precision=highest) - jnp.dot(left[1], right[1], precision=highest)
    imag_part = jnp.dot(left[0], right[1], precision=highest) + jnp.dot(left[1], right[0], precision=highest)
    return jnp.stack([real_part, imag_part])

def reference(seismic, band_low, band_high, leaf_weights, translations, level_table):
    highest = lax.Precision.HIGHEST
    dft_rows = spectral_table(F, NT)
    dft_wide = dft_rows.astype(jnp.float32)
    freq_index = jnp.arange(F, dtype=jnp.int32)
    band_mask = ((freq_index[:, None] >= band_low[None, :]) & (freq_index[:, None] < band_high[None, :])).astype(jnp.bfloat16)
    blocks = seismic.reshape(N_TRACE, N_SPACE, N_SUB, TR_DEV, NT, SHOTS)

    def accumulate(carry, block):
        spectra = jnp.einsum('kt,puxts->puxks', dft_wide, block.astype(jnp.float32), precision=highest)
        spectra = spectra.astype(jnp.bfloat16).reshape(N_SPACE, N_SUB, TR_DEV, 2, F, SHOTS) * band_mask
        return (carry + lax.optimization_barrier(jnp.sum(spectra.astype(jnp.float32), axis=1)), None)
    start_sum = jnp.zeros((N_SPACE, TR_DEV, 2, F, SHOTS), jnp.float32)
    summed, _ = lax.scan(accumulate, start_sum, blocks)
    freq_block = F // N_TRACE
    banded = summed.reshape(N_SPACE, TR_DEV, 2, N_TRACE, freq_block, SHOTS)
    leaf_wide = leaf_weights.astype(jnp.float32).reshape(TR_DEV, N_TRACE, freq_block, 2, R)
    parts = jnp.einsum('piagfs,igfbr->gpabrs', banded, leaf_wide, precision=highest)
    real_part = parts[:, :, 0, 0] - parts[:, :, 1, 1]
    imag_part = parts[:, :, 0, 1] + parts[:, :, 1, 0]
    weights_now = jnp.stack([real_part, imag_part], axis=2).reshape(N_TRACE * N_SPACE, 2, R, SHOTS)
    box_index = jnp.arange(N_TRACE * N_SPACE, dtype=jnp.int32)
    for section_no in range(SPACE_BITS + TRACE_BITS):
        stride = 2 ** section_no
        lower_box = box_index - box_index // stride % 2 * stride
        upper_box = lower_box + stride
        first_mats = translations[level_table[section_no, :, 0]]
        second_mats = translations[level_table[section_no, :, 1]]
        weights_now = jax.vmap(complex_product)(first_mats, weights_now[lower_box]) + jax.vmap(complex_product)(second_mats, weights_now[upper_box])
    return weights_now
```

```python
import functools
import math

import jax
import jax.numpy as jnp
import ml_dtypes
import numpy as np
from jax import lax
from jax.experimental import pallas as pl
from jax.experimental.pallas import tpu as pltpu
from jax.sharding import PartitionSpec as P

LANES = 128


def swapped(x, axis, distance):
    return lax.ppermute(x, axis, [(i, i ^ 1 << distance) for i in range(lax.axis_size(axis))])


def spectral_table(freq_total, samples):
    freq_range = jnp.arange(freq_total, dtype=jnp.int32)
    time_range = jnp.arange(samples, dtype=jnp.int32)
    phase = freq_range[:, None] * time_range[None, :] % samples
    angle = phase.astype(jnp.float32) * (2.0 * math.pi / samples)
    factor = 1.0 / math.sqrt(samples)
    return (jnp.concatenate([jnp.cos(angle), -jnp.sin(angle)], axis=0) * factor).astype(
        jnp.bfloat16
    )


def complex_product(left, right):
    highest = lax.Precision.HIGHEST
    real_part = jnp.dot(left[0], right[0], precision=highest) - jnp.dot(
        left[1], right[1], precision=highest
    )
    imag_part = jnp.dot(left[0], right[1], precision=highest) + jnp.dot(
        left[1], right[0], precision=highest
    )
    return jnp.stack([real_part, imag_part])


def swap_space(weights_now, bit_no):
    return swapped(weights_now, "space", bit_no)


def swap_trace(weights_now, bit_no):
    return swapped(weights_now, "trace", bit_no)


def merge_level(
    weights_now, partner, section_no, box_index, translations, level_table, sub_place, half_rank
):
    stride = 2**section_no
    upper_flag = box_index // stride % 2 == 1
    lower_part = jnp.where(upper_flag, partner, weights_now)
    upper_part = jnp.where(upper_flag, weights_now, partner)
    entries = lax.dynamic_index_in_dim(level_table[section_no], box_index, 0, keepdims=False)
    first_mat = lax.dynamic_index_in_dim(translations, entries[0], 0, keepdims=False)
    second_mat = lax.dynamic_index_in_dim(translations, entries[1], 0, keepdims=False)
    full_lower, full_upper = (
        lax.all_gather(lower_part, "sub", axis=1, tiled=True),
        lax.all_gather(upper_part, "sub", axis=1, tiled=True),
    )
    first_rows = lax.dynamic_slice_in_dim(first_mat, sub_place * half_rank, half_rank, 1)
    second_rows = lax.dynamic_slice_in_dim(second_mat, sub_place * half_rank, half_rank, 1)
    return complex_product(first_rows, full_lower) + complex_product(second_rows, full_upper)


def join_complex(parts):
    return jnp.stack([parts[:, 0, 0] - parts[:, 1, 1], parts[:, 0, 1] + parts[:, 1, 0]], axis=1)


def general_device(seismic, band_low, band_high, leaf_weights, translations, level_table):
    highest = lax.Precision.HIGHEST
    trace_count = lax.axis_size("trace")
    space_count = lax.axis_size("space")
    sub_count = lax.axis_size("sub")
    trace_place = lax.axis_index("trace")
    space_place = lax.axis_index("space")
    sub_place = lax.axis_index("sub")
    traces_here = seismic.shape[0]
    samples = seismic.shape[1]
    shots_count = seismic.shape[2]
    freq_total = leaf_weights.shape[1]
    rank_total = leaf_weights.shape[3]
    freq_block = freq_total // trace_count
    half_rank = rank_total // sub_count
    dft_rows = spectral_table(freq_total, samples)
    spectra = jnp.einsum(
        "kt,xts->xks", dft_rows, seismic, preferred_element_type=jnp.float32
    ).astype(jnp.bfloat16)
    spectra = spectra.reshape(traces_here, 2, freq_total, shots_count)
    freq_index = jnp.arange(freq_total, dtype=jnp.int32)
    band_mask = (
        (freq_index[:, None] >= band_low[None, :]) & (freq_index[:, None] < band_high[None, :])
    ).astype(jnp.bfloat16)
    masked = spectra * band_mask
    piece = masked.astype(jnp.float32)
    piece = piece.reshape(traces_here, 2, 1 * lax.axis_size("trace"), freq_block, shots_count)
    leaf_piece = leaf_weights.astype(jnp.float32)
    leaf_piece = leaf_piece.reshape(
        traces_here, 1 * lax.axis_size("trace"), freq_block, 2, rank_total
    )
    parts = jnp.einsum("iagfs,igfbr->gabrs", piece, leaf_piece, precision=highest)
    leaf_terms = lax.psum_scatter(join_complex(parts), "trace", scatter_dimension=0, tiled=True)[0]
    weights_now = lax.psum_scatter(leaf_terms, "sub", scatter_dimension=1, tiled=True)
    box_index = trace_place * space_count + space_place
    section_no = 0
    for bit_no in range(space_count.bit_length() - 1):
        partner = swap_space(weights_now, bit_no)
        weights_now = merge_level(
            weights_now,
            partner,
            section_no,
            box_index,
            translations,
            level_table,
            sub_place,
            half_rank,
        )
        section_no = section_no + 1
    for bit_no in range(trace_count.bit_length() - 1):
        partner = swap_trace(weights_now, bit_no)
        weights_now = merge_level(
            weights_now,
            partner,
            section_no,
            box_index,
            translations,
            level_table,
            sub_place,
            half_rank,
        )
        section_no = section_no + 1
    return weights_now[None]


def table_rows(freq_total, samples, chunks):
    phase = np.arange(freq_total)[:, None] * np.arange(samples)[None, :] % samples
    angle = phase.astype(np.float32) * np.float32(2.0 * math.pi / samples)
    factor = np.float32(1.0 / math.sqrt(samples))
    parts = np.stack([np.cos(angle), -np.sin(angle)]) * factor
    rows = parts.reshape(2, chunks, freq_total // chunks, samples).transpose(1, 0, 2, 3)
    return rows.reshape(chunks, 2 * freq_total // chunks, samples).astype(ml_dtypes.bfloat16)


def split_two(x):
    high = x.astype(jnp.bfloat16).astype(jnp.float32)
    return high, x - high


def fused_kernel(
    sizes,
    x_hbm,
    low_ref,
    high_ref,
    q_hbm,
    tab_hbm,
    tr_hbm,
    level_ref,
    out_ref,
    x_v,
    q_v,
    tab_v,
    tr_v,
    spec_v,
    mat_hi,
    mat_lo,
    send1,
    recv1,
    send2,
    recv2,
    load_sem,
    send_sem1,
    recv_sem1,
    send_sem2,
    recv_sem2,
):
    trace_count, space_count, sub_count = sizes
    devices = trace_count * space_count * sub_count
    t, p, u = lax.axis_index("trace"), lax.axis_index("space"), lax.axis_index("sub")
    me = (t * space_count + p) * sub_count + u
    chunks = tab_v.shape[0]
    traces = q_v.shape[0]
    pairs = traces // 2
    bands = trace_count // chunks
    boxes = trace_count * space_count
    levels = mat_hi.shape[0]
    rank = tr_v.shape[2]
    half = rank // sub_count
    block = LANES // devices

    loads = []
    for h in range(chunks):
        loads.append(pltpu.make_async_copy(tab_hbm.at[h], tab_v.at[h], load_sem.at[len(loads)]))
    x_loads = []
    for j in range(traces):
        x_loads.append(
            pltpu.make_async_copy(
                x_hbm.at[j],
                x_v.at[j // 2, :, pl.ds(j % 2 * LANES, LANES)],
                load_sem.at[chunks + j],
            )
        )
    q_load = pltpu.make_async_copy(q_hbm, q_v, load_sem.at[chunks + traces])
    tr_load = pltpu.make_async_copy(tr_hbm, tr_v, load_sem.at[chunks + traces + 1])
    loads[0].start()
    for load in x_loads:
        load.start()
    q_load.start()
    for load in loads[1:]:
        load.start()
    tr_load.start()

    offsets = [
        (dt, dp, du)
        for dt in range(trace_count)
        for dp in range(space_count)
        for du in range(sub_count)
        if dt or dp or du
    ]
    offsets.sort(key=lambda o: -min(o[0], trace_count - o[0]) * 4 - o[1] * 2 - o[2])

    def place(offset):
        dt, dp, du = offset
        tt = lax.rem(t + dt, trace_count)
        pp = lax.rem(p + dp, space_count)
        uu = lax.rem(u + du, sub_count)
        return tt, pp, uu

    barrier = pltpu.get_barrier_semaphore()
    for offset in offsets:
        tt, pp, uu = place(offset)
        pl.semaphore_signal(
            barrier,
            inc=1,
            device_id={"trace": tt, "space": pp, "sub": uu},
            device_id_type=pl.DeviceIdType.MESH,
        )

    copies1 = []
    for h in range(chunks):
        loads[h].wait()
        width = bands * LANES
        freq = lax.broadcasted_iota(jnp.int32, (width, LANES), 0) + h * width
        keep = (freq >= low_ref[...]) & (freq < high_ref[...])
        for pair in range(pairs):
            if h == 0:
                x_loads[2 * pair].wait()
                x_loads[2 * pair + 1].wait()
            rows = jnp.dot(tab_v[h], x_v[pair], preferred_element_type=jnp.float32)
            for part in range(2):
                for k in range(2):
                    piece = rows[part * width : (part + 1) * width, k * LANES : (k + 1) * LANES]
                    piece = jnp.where(keep, piece, 0.0).astype(jnp.bfloat16)
                    j = 2 * pair + k
                    for g in range(bands):
                        spec_v[
                            h * bands + g,
                            j * LANES : (j + 1) * LANES,
                            part * LANES : (part + 1) * LANES,
                        ] = piece[g * LANES : (g + 1) * LANES]
        if h == 0:
            q_load.wait()
        leaves = []
        for g in range(h * bands, (h + 1) * bands):
            left = jnp.concatenate(
                [q_v[j, :, g * LANES : (g + 1) * LANES] for j in range(traces)], axis=1
            )
            both = jnp.dot(left, spec_v[g], preferred_element_type=jnp.float32)
            real = both[:rank, :LANES] - both[rank:, LANES:]
            imag = both[rank:, :LANES] + both[:rank, LANES:]
            turned = jnp.concatenate([real, imag], axis=0).T
            leaves.append(turned.reshape(devices, block, LANES))
        send1[h] = jnp.concatenate(leaves, axis=1).astype(jnp.bfloat16)
        if h == 0:
            pl.semaphore_wait(barrier, devices - 1)
        for i, offset in enumerate(offsets):
            tt, pp, uu = place(offset)
            copy = pltpu.make_async_remote_copy(
                src_ref=send1.at[h, (tt * space_count + pp) * sub_count + uu],
                dst_ref=recv1.at[h, i],
                send_sem=send_sem1.at[h, i],
                recv_sem=recv_sem1.at[h, i],
                device_id={"trace": tt, "space": pp, "sub": uu},
                device_id_type=pl.DeviceIdType.MESH,
            )
            copy.start()
            copies1.append(copy)

    tr_load.wait()
    for level in range(levels):
        stride = 2**level
        lowers = [b for b in range(boxes) if b // stride % 2 == 0]
        for q, lower in enumerate(lowers):
            for side in range(2):
                for child in range(2):
                    entry = level_ref[level, child, lower + side * stride]
                    real, imag = tr_v[entry, 0], tr_v[entry, 1]
                    top = jnp.concatenate([real, -imag], axis=1)
                    bottom = jnp.concatenate([imag, real], axis=1)
                    for part, rows in enumerate((top, bottom)):
                        high, rest = split_two(rows)
                        high, rest = high.astype(jnp.bfloat16), rest.astype(jnp.bfloat16)
                        columns = slice(child * LANES, (child + 1) * LANES)
                        if level < levels - 1:
                            at = side * 2 * rank + part * rank
                            mat_hi[level, q, at : at + rank, columns] = high
                            mat_lo[level, q, at : at + rank, columns] = rest
                        else:
                            for s in range(sub_count):
                                at = s * 4 * half + side * 2 * half + part * half
                                mine = slice(s * half, (s + 1) * half)
                                mat_hi[level, q, at : at + half, columns] = high[mine]
                                mat_lo[level, q, at : at + half, columns] = rest[mine]

    same = [send1[h, me].astype(jnp.float32) for h in range(chunks)]
    other = [None] * chunks
    for h in range(chunks):
        for i, offset in enumerate(offsets):
            copies1[h * len(offsets) + i].wait_recv()
            got = recv1[h, i].astype(jnp.float32)
            if offset[1] == 0:
                same[h] = same[h] + got
            else:
                other[h] = got if other[h] is None else other[h] + got
    first = p == 0
    now = [None] * boxes
    for h in range(chunks):
        for place_no in range(space_count):
            total = jnp.where(first == (place_no == 0), same[h], other[h])
            for g in range(bands):
                box = (h * bands + g) * space_count + place_no
                now[box] = total[g * block : (g + 1) * block]

    for level in range(levels):
        stride = 2**level
        lowers = [b for b in range(boxes) if b // stride % 2 == 0]
        for q, lower in enumerate(lowers):
            both = jnp.concatenate([now[lower], now[lower + stride]], axis=1)
            left = jnp.concatenate(split_two(both), axis=0).astype(jnp.bfloat16)
            dims = (((1,), (1,)), ((), ()))
            main = lax.dot_general(
                left, mat_hi[level, q], dims, preferred_element_type=jnp.float32
            )
            rest = lax.dot_general(
                left, mat_lo[level, q], dims, preferred_element_type=jnp.float32
            )
            joined = main[:block] + (main[block:] + rest[:block])
            if level < levels - 1:
                now[lower], now[lower + stride] = joined[:, :LANES], joined[:, LANES:]
            else:
                for s in range(sub_count):
                    send2[q * sub_count + s] = joined[:, s * LANES : (s + 1) * LANES]

    copies2 = []
    for i, offset in enumerate(offsets):
        tt, pp, uu = place(offset)
        copy = pltpu.make_async_remote_copy(
            src_ref=send2.at[lax.rem(tt * space_count + pp, boxes // 2) * sub_count + uu],
            dst_ref=recv2.at[me],
            send_sem=send_sem2.at[i],
            recv_sem=recv_sem2.at[i],
            device_id={"trace": tt, "space": pp, "sub": uu},
            device_id_type=pl.DeviceIdType.MESH,
        )
        copy.start()
        copies2.append(copy)
    mine = t * space_count + p
    recv2[me] = send2[lax.rem(mine, boxes // 2) * sub_count + u]
    for copy in copies2:
        copy.wait_recv()
    turned = recv2[...].reshape(LANES, LANES).T
    upper = mine >= boxes // 2
    chosen = jnp.where(upper, turned[2 * half :], turned[: 2 * half])
    out_ref[...] = chosen.reshape(1, 2, half, LANES)
    for copy in copies1 + copies2:
        copy.wait_send()


def fused_device(seismic, band_low, band_high, leaf_weights, translations, level_table):
    sizes = tuple(lax.axis_size(name) for name in ("trace", "space", "sub"))
    devices = math.prod(sizes)
    boxes = sizes[0] * sizes[1]
    traces, samples, shots = seismic.shape
    freq_total, rank = leaf_weights.shape[1], leaf_weights.shape[3]
    chunks = 2
    levels = level_table.shape[0]
    table = jnp.asarray(table_rows(freq_total, samples, chunks))
    weights = leaf_weights.transpose(0, 2, 3, 1).reshape(traces, 2 * rank, freq_total)
    block = shots // devices
    rows = sizes[0] // chunks * block
    any_spec = pl.BlockSpec(memory_space=pl.ANY)
    vmem_spec = pl.BlockSpec(memory_space=pltpu.VMEM)
    dma = pltpu.SemaphoreType.DMA
    return pl.pallas_call(
        functools.partial(fused_kernel, sizes),
        out_shape=jax.ShapeDtypeStruct((1, 2, rank // sizes[2], shots), jnp.float32),
        in_specs=[
            any_spec,
            vmem_spec,
            vmem_spec,
            any_spec,
            any_spec,
            any_spec,
            pl.BlockSpec(memory_space=pltpu.SMEM),
        ],
        out_specs=vmem_spec,
        scratch_shapes=[
            pltpu.VMEM((traces // 2, samples, 2 * shots), jnp.bfloat16),
            pltpu.VMEM(weights.shape, jnp.bfloat16),
            pltpu.VMEM(table.shape, jnp.bfloat16),
            pltpu.VMEM(translations.shape, jnp.float32),
            pltpu.VMEM((sizes[0], traces * LANES, 2 * LANES), jnp.bfloat16),
            pltpu.VMEM((levels, boxes // 2, 4 * rank, 4 * rank), jnp.bfloat16),
            pltpu.VMEM((levels, boxes // 2, 4 * rank, 4 * rank), jnp.bfloat16),
            pltpu.VMEM((chunks, devices, rows, LANES), jnp.bfloat16),
            pltpu.VMEM((chunks, devices - 1, rows, LANES), jnp.bfloat16),
            pltpu.VMEM((boxes // 2 * sizes[2], block, LANES), jnp.float32),
            pltpu.VMEM((devices, block, LANES), jnp.float32),
            dma((chunks + traces + 2,)),
            dma((chunks, devices - 1)),
            dma((chunks, devices - 1)),
            dma((devices - 1,)),
            dma((devices - 1,)),
        ],
        compiler_params=pltpu.CompilerParams(
            collective_id=0, has_side_effects=True, vmem_limit_bytes=40 * 2**20
        ),
    )(
        seismic,
        band_low.reshape(1, shots),
        band_high.reshape(1, shots),
        weights,
        table,
        translations,
        level_table.transpose(0, 2, 1),
    )


def per_device(seismic, band_low, band_high, leaf_weights, translations, level_table):
    trace_count, space_count, sub_count = (
        lax.axis_size(name) for name in ("trace", "space", "sub")
    )
    devices = trace_count * space_count * sub_count
    traces, _, shots = seismic.shape
    freq_total, rank = leaf_weights.shape[1], leaf_weights.shape[3]
    fits = (
        shots == LANES
        and shots == 8 * devices
        and freq_total == trace_count * LANES
        and 2 * rank == LANES
        and 4 * rank == LANES * sub_count
        and traces % 2 == 0
        and trace_count % 2 == 0
    )
    chosen = fused_device if fits else general_device
    return chosen(seismic, band_low, band_high, leaf_weights, translations, level_table)


def solution(mesh):
    placed = (
        P(("groups", "trace", "space", "sub"), None, None),
        P("groups"),
        P("groups"),
        P(),
        P(),
        P(),
    )
    return jax.shard_map(
        per_device,
        mesh=mesh,
        in_specs=placed,
        out_specs=P(("groups", "trace", "space"), None, "sub", None),
        check_vma=False,
    )
```

```python
import functools
import math

import jax
import jax.numpy as jnp
import ml_dtypes
import numpy as np
from jax import lax
from jax.experimental import pallas as pl
from jax.experimental.pallas import tpu as pltpu
from jax.sharding import PartitionSpec as P

LANES = 128


def swapped(x, axis, distance):
    return lax.ppermute(x, axis, [(i, i ^ 1 << distance) for i in range(lax.axis_size(axis))])


def spectral_table(freq_total, samples):
    freq_range = jnp.arange(freq_total, dtype=jnp.int32)
    time_range = jnp.arange(samples, dtype=jnp.int32)
    phase = freq_range[:, None] * time_range[None, :] % samples
    angle = phase.astype(jnp.float32) * (2.0 * math.pi / samples)
    factor = 1.0 / math.sqrt(samples)
    return (jnp.concatenate([jnp.cos(angle), -jnp.sin(angle)], axis=0) * factor).astype(
        jnp.bfloat16
    )


def complex_product(left, right):
    highest = lax.Precision.HIGHEST
    real_part = jnp.dot(left[0], right[0], precision=highest) - jnp.dot(
        left[1], right[1], precision=highest
    )
    imag_part = jnp.dot(left[0], right[1], precision=highest) + jnp.dot(
        left[1], right[0], precision=highest
    )
    return jnp.stack([real_part, imag_part])


def swap_space(weights_now, bit_no):
    return swapped(weights_now, "space", bit_no)


def swap_trace(weights_now, bit_no):
    return swapped(weights_now, "trace", bit_no)


def merge_level(
    weights_now, partner, section_no, box_index, translations, level_table, sub_place, half_rank
):
    stride = 2**section_no
    upper_flag = box_index // stride % 2 == 1
    lower_part = jnp.where(upper_flag, partner, weights_now)
    upper_part = jnp.where(upper_flag, weights_now, partner)
    entries = lax.dynamic_index_in_dim(level_table[section_no], box_index, 0, keepdims=False)
    first_mat = lax.dynamic_index_in_dim(translations, entries[0], 0, keepdims=False)
    second_mat = lax.dynamic_index_in_dim(translations, entries[1], 0, keepdims=False)
    full_lower, full_upper = (
        lax.all_gather(lower_part, "sub", axis=1, tiled=True),
        lax.all_gather(upper_part, "sub", axis=1, tiled=True),
    )
    first_rows = lax.dynamic_slice_in_dim(first_mat, sub_place * half_rank, half_rank, 1)
    second_rows = lax.dynamic_slice_in_dim(second_mat, sub_place * half_rank, half_rank, 1)
    return complex_product(first_rows, full_lower) + complex_product(second_rows, full_upper)


def join_complex(parts):
    return jnp.stack([parts[:, 0, 0] - parts[:, 1, 1], parts[:, 0, 1] + parts[:, 1, 0]], axis=1)


def general_device(seismic, band_low, band_high, leaf_weights, translations, level_table):
    highest = lax.Precision.HIGHEST
    trace_count = lax.axis_size("trace")
    space_count = lax.axis_size("space")
    sub_count = lax.axis_size("sub")
    trace_place = lax.axis_index("trace")
    space_place = lax.axis_index("space")
    sub_place = lax.axis_index("sub")
    traces_here = seismic.shape[0]
    samples = seismic.shape[1]
    shots_count = seismic.shape[2]
    freq_total = leaf_weights.shape[1]
    rank_total = leaf_weights.shape[3]
    freq_block = freq_total // trace_count
    half_rank = rank_total // sub_count
    dft_rows = spectral_table(freq_total, samples)
    spectra = jnp.einsum(
        "kt,xts->xks", dft_rows, seismic, preferred_element_type=jnp.float32
    ).astype(jnp.bfloat16)
    spectra = spectra.reshape(traces_here, 2, freq_total, shots_count)
    freq_index = jnp.arange(freq_total, dtype=jnp.int32)
    band_mask = (
        (freq_index[:, None] >= band_low[None, :]) & (freq_index[:, None] < band_high[None, :])
    ).astype(jnp.bfloat16)
    masked = spectra * band_mask
    piece = masked.astype(jnp.float32)
    piece = piece.reshape(traces_here, 2, 1 * lax.axis_size("trace"), freq_block, shots_count)
    leaf_piece = leaf_weights.astype(jnp.float32)
    leaf_piece = leaf_piece.reshape(
        traces_here, 1 * lax.axis_size("trace"), freq_block, 2, rank_total
    )
    parts = jnp.einsum("iagfs,igfbr->gabrs", piece, leaf_piece, precision=highest)
    leaf_terms = lax.psum_scatter(join_complex(parts), "trace", scatter_dimension=0, tiled=True)[0]
    weights_now = lax.psum_scatter(leaf_terms, "sub", scatter_dimension=1, tiled=True)
    box_index = trace_place * space_count + space_place
    section_no = 0
    for bit_no in range(space_count.bit_length() - 1):
        partner = swap_space(weights_now, bit_no)
        weights_now = merge_level(
            weights_now,
            partner,
            section_no,
            box_index,
            translations,
            level_table,
            sub_place,
            half_rank,
        )
        section_no = section_no + 1
    for bit_no in range(trace_count.bit_length() - 1):
        partner = swap_trace(weights_now, bit_no)
        weights_now = merge_level(
            weights_now,
            partner,
            section_no,
            box_index,
            translations,
            level_table,
            sub_place,
            half_rank,
        )
        section_no = section_no + 1
    return weights_now[None]


def table_rows(freq_total, samples, chunks):
    phase = np.arange(freq_total)[:, None] * np.arange(samples)[None, :] % samples
    angle = phase.astype(np.float32) * np.float32(2.0 * math.pi / samples)
    factor = np.float32(1.0 / math.sqrt(samples))
    parts = np.stack([np.cos(angle), -np.sin(angle)]) * factor
    rows = parts.reshape(2, chunks, freq_total // chunks, samples).transpose(1, 0, 2, 3)
    return rows.reshape(chunks, 2 * freq_total // chunks, samples).astype(ml_dtypes.bfloat16)


def split_two(x):
    high = x.astype(jnp.bfloat16).astype(jnp.float32)
    return high, x - high


def fused_kernel(
    sizes,
    x_hbm,
    low_hbm,
    high_hbm,
    q_hbm,
    tab_hbm,
    tr_hbm,
    level_hbm,
    out_ref,
    band_v,
    level_ref,
    x_v,
    q_v,
    tab_v,
    tr_v,
    spec_v,
    mat_hi,
    mat_lo,
    send1,
    recv1,
    send2,
    recv2,
    load_sem,
    small_sem,
    send_sem1,
    recv_sem1,
    send_sem2,
    recv_sem2,
):
    trace_count, space_count, sub_count = sizes
    devices = trace_count * space_count * sub_count
    t, p, u = lax.axis_index("trace"), lax.axis_index("space"), lax.axis_index("sub")
    me = (t * space_count + p) * sub_count + u
    chunks = tab_v.shape[0]
    traces = q_v.shape[0]
    pairs = traces // 2
    bands = trace_count // chunks
    boxes = trace_count * space_count
    levels = mat_hi.shape[0]
    rank = tr_v.shape[2]
    half = rank // sub_count
    block = LANES // devices

    band_loads = [
        pltpu.make_async_copy(low_hbm, band_v.at[0], small_sem.at[0]),
        pltpu.make_async_copy(high_hbm, band_v.at[1], small_sem.at[1]),
    ]
    level_load = pltpu.make_async_copy(level_hbm, level_ref, small_sem.at[2])
    loads = []
    for h in range(chunks):
        loads.append(pltpu.make_async_copy(tab_hbm.at[h], tab_v.at[h], load_sem.at[len(loads)]))
    x_loads = []
    for j in range(traces):
        x_loads.append(
            pltpu.make_async_copy(
                x_hbm.at[j],
                x_v.at[j // 2, :, pl.ds(j % 2 * LANES, LANES)],
                load_sem.at[chunks + j],
            )
        )
    q_load = pltpu.make_async_copy(q_hbm, q_v, load_sem.at[chunks + traces])
    tr_load = pltpu.make_async_copy(tr_hbm, tr_v, load_sem.at[chunks + traces + 1])
    loads[0].start()
    for load in x_loads:
        load.start()
    for load in band_loads:
        load.start()
    q_load.start()
    for load in loads[1:]:
        load.start()
    level_load.start()
    tr_load.start()

    offsets = [
        (dt, dp, du)
        for dt in range(trace_count)
        for dp in range(space_count)
        for du in range(sub_count)
        if dt or dp or du
    ]
    offsets.sort(key=lambda o: -min(o[0], trace_count - o[0]) * 4 - o[1] * 2 - o[2])

    def place(offset):
        dt, dp, du = offset
        tt = lax.rem(t + dt, trace_count)
        pp = lax.rem(p + dp, space_count)
        uu = lax.rem(u + du, sub_count)
        return tt, pp, uu

    barrier = pltpu.get_barrier_semaphore()
    for offset in offsets:
        tt, pp, uu = place(offset)
        pl.semaphore_signal(
            barrier,
            inc=1,
            device_id={"trace": tt, "space": pp, "sub": uu},
            device_id_type=pl.DeviceIdType.MESH,
        )

    copies1 = []
    for h in range(chunks):
        loads[h].wait()
        width = bands * LANES
        freq = lax.broadcasted_iota(jnp.int32, (width, LANES), 0) + h * width
        if h == 0:
            for load in band_loads:
                load.wait()
        keep = (freq >= band_v[0]) & (freq < band_v[1])
        for pair in range(pairs):
            if h == 0:
                x_loads[2 * pair].wait()
                x_loads[2 * pair + 1].wait()
            rows = jnp.dot(tab_v[h], x_v[pair], preferred_element_type=jnp.float32)
            for part in range(2):
                for k in range(2):
                    piece = rows[part * width : (part + 1) * width, k * LANES : (k + 1) * LANES]
                    piece = jnp.where(keep, piece, 0.0).astype(jnp.bfloat16)
                    j = 2 * pair + k
                    for g in range(bands):
                        spec_v[
                            h * bands + g,
                            j * LANES : (j + 1) * LANES,
                            part * LANES : (part + 1) * LANES,
                        ] = piece[g * LANES : (g + 1) * LANES]
        if h == 0:
            q_load.wait()
        leaves = []
        for g in range(h * bands, (h + 1) * bands):
            left = jnp.concatenate(
                [q_v[j, :, g * LANES : (g + 1) * LANES] for j in range(traces)], axis=1
            )
            both = jnp.dot(left, spec_v[g], preferred_element_type=jnp.float32)
            real = both[:rank, :LANES] - both[rank:, LANES:]
            imag = both[rank:, :LANES] + both[:rank, LANES:]
            turned = jnp.concatenate([real, imag], axis=0).T
            leaves.append(turned.reshape(devices, block, LANES))
        send1[h] = jnp.concatenate(leaves, axis=1).astype(jnp.bfloat16)
        if h == 0:
            pl.semaphore_wait(barrier, devices - 1)
        for i, offset in enumerate(offsets):
            tt, pp, uu = place(offset)
            copy = pltpu.make_async_remote_copy(
                src_ref=send1.at[h, (tt * space_count + pp) * sub_count + uu],
                dst_ref=recv1.at[h, i],
                send_sem=send_sem1.at[h, i],
                recv_sem=recv_sem1.at[h, i],
                device_id={"trace": tt, "space": pp, "sub": uu},
                device_id_type=pl.DeviceIdType.MESH,
            )
            copy.start()
            copies1.append(copy)

    level_load.wait()
    tr_load.wait()
    for level in range(levels):
        stride = 2**level
        lowers = [b for b in range(boxes) if b // stride % 2 == 0]
        for q, lower in enumerate(lowers):
            for side in range(2):
                for child in range(2):
                    entry = level_ref[level, child, lower + side * stride]
                    real, imag = tr_v[entry, 0], tr_v[entry, 1]
                    top = jnp.concatenate([real, -imag], axis=1)
                    bottom = jnp.concatenate([imag, real], axis=1)
                    for part, rows in enumerate((top, bottom)):
                        high, rest = split_two(rows)
                        high, rest = high.astype(jnp.bfloat16), rest.astype(jnp.bfloat16)
                        columns = slice(child * LANES, (child + 1) * LANES)
                        if level < levels - 1:
                            at = side * 2 * rank + part * rank
                            mat_hi[level, q, at : at + rank, columns] = high
                            mat_lo[level, q, at : at + rank, columns] = rest
                        else:
                            for s in range(sub_count):
                                at = s * 4 * half + side * 2 * half + part * half
                                mine = slice(s * half, (s + 1) * half)
                                mat_hi[level, q, at : at + half, columns] = high[mine]
                                mat_lo[level, q, at : at + half, columns] = rest[mine]

    same = [send1[h, me].astype(jnp.float32) for h in range(chunks)]
    other = [None] * chunks
    for h in range(chunks):
        for i, offset in enumerate(offsets):
            copies1[h * len(offsets) + i].wait_recv()
            got = recv1[h, i].astype(jnp.float32)
            if offset[1] == 0:
                same[h] = same[h] + got
            else:
                other[h] = got if other[h] is None else other[h] + got
    first = p == 0
    now = [None] * boxes
    for h in range(chunks):
        for place_no in range(space_count):
            total = jnp.where(first == (place_no == 0), same[h], other[h])
            for g in range(bands):
                box = (h * bands + g) * space_count + place_no
                now[box] = total[g * block : (g + 1) * block]

    for level in range(levels):
        stride = 2**level
        lowers = [b for b in range(boxes) if b // stride % 2 == 0]
        for q, lower in enumerate(lowers):
            both = jnp.concatenate([now[lower], now[lower + stride]], axis=1)
            left = jnp.concatenate(split_two(both), axis=0).astype(jnp.bfloat16)
            dims = (((1,), (1,)), ((), ()))
            main = lax.dot_general(
                left, mat_hi[level, q], dims, preferred_element_type=jnp.float32
            )
            rest = lax.dot_general(
                left, mat_lo[level, q], dims, preferred_element_type=jnp.float32
            )
            joined = main[:block] + (main[block:] + rest[:block])
            if level < levels - 1:
                now[lower], now[lower + stride] = joined[:, :LANES], joined[:, LANES:]
            else:
                for s in range(sub_count):
                    send2[q * sub_count + s] = joined[:, s * LANES : (s + 1) * LANES]

    copies2 = []
    for i, offset in enumerate(offsets):
        tt, pp, uu = place(offset)
        copy = pltpu.make_async_remote_copy(
            src_ref=send2.at[lax.rem(tt * space_count + pp, boxes // 2) * sub_count + uu],
            dst_ref=recv2.at[me],
            send_sem=send_sem2.at[i],
            recv_sem=recv_sem2.at[i],
            device_id={"trace": tt, "space": pp, "sub": uu},
            device_id_type=pl.DeviceIdType.MESH,
        )
        copy.start()
        copies2.append(copy)
    mine = t * space_count + p
    recv2[me] = send2[lax.rem(mine, boxes // 2) * sub_count + u]
    for copy in copies2:
        copy.wait_recv()
    turned = recv2[...].reshape(LANES, LANES).T
    upper = mine >= boxes // 2
    chosen = jnp.where(upper, turned[2 * half :], turned[: 2 * half])
    out_ref[...] = chosen.reshape(1, 2, half, LANES)
    for copy in copies1 + copies2:
        copy.wait_send()


def fused_device(seismic, band_low, band_high, leaf_weights, translations, level_table):
    sizes = tuple(lax.axis_size(name) for name in ("trace", "space", "sub"))
    devices = math.prod(sizes)
    boxes = sizes[0] * sizes[1]
    traces, samples, shots = seismic.shape
    freq_total, rank = leaf_weights.shape[1], leaf_weights.shape[3]
    chunks = 2
    levels = level_table.shape[0]
    table = jnp.asarray(table_rows(freq_total, samples, chunks))
    weights = leaf_weights.transpose(0, 2, 3, 1).reshape(traces, 2 * rank, freq_total)
    block = shots // devices
    rows = sizes[0] // chunks * block
    hbm_spec = pl.BlockSpec(memory_space=pltpu.HBM)
    vmem_spec = pl.BlockSpec(memory_space=pltpu.VMEM)
    dma = pltpu.SemaphoreType.DMA
    return pl.pallas_call(
        functools.partial(fused_kernel, sizes),
        out_shape=jax.ShapeDtypeStruct((1, 2, rank // sizes[2], shots), jnp.float32),
        in_specs=[hbm_spec] * 7,
        out_specs=vmem_spec,
        scratch_shapes=[
            pltpu.VMEM((2, 1, shots), jnp.int32),
            pltpu.SMEM((levels, 2, boxes), jnp.int32),
            pltpu.VMEM((traces // 2, samples, 2 * shots), jnp.bfloat16),
            pltpu.VMEM(weights.shape, jnp.bfloat16),
            pltpu.VMEM(table.shape, jnp.bfloat16),
            pltpu.VMEM(translations.shape, jnp.float32),
            pltpu.VMEM((sizes[0], traces * LANES, 2 * LANES), jnp.bfloat16),
            pltpu.VMEM((levels, boxes // 2, 4 * rank, 4 * rank), jnp.bfloat16),
            pltpu.VMEM((levels, boxes // 2, 4 * rank, 4 * rank), jnp.bfloat16),
            pltpu.VMEM((chunks, devices, rows, LANES), jnp.bfloat16),
            pltpu.VMEM((chunks, devices - 1, rows, LANES), jnp.bfloat16),
            pltpu.VMEM((boxes // 2 * sizes[2], block, LANES), jnp.float32),
            pltpu.VMEM((devices, block, LANES), jnp.float32),
            dma((chunks + traces + 2,)),
            dma((3,)),
            dma((chunks, devices - 1)),
            dma((chunks, devices - 1)),
            dma((devices - 1,)),
            dma((devices - 1,)),
        ],
        compiler_params=pltpu.CompilerParams(
            collective_id=0, has_side_effects=True, vmem_limit_bytes=56 * 2**20
        ),
    )(
        seismic,
        band_low.reshape(1, shots),
        band_high.reshape(1, shots),
        weights,
        table,
        translations,
        level_table.transpose(0, 2, 1),
    )


def per_device(seismic, band_low, band_high, leaf_weights, translations, level_table):
    trace_count, space_count, sub_count = (
        lax.axis_size(name) for name in ("trace", "space", "sub")
    )
    devices = trace_count * space_count * sub_count
    traces, _, shots = seismic.shape
    freq_total, rank = leaf_weights.shape[1], leaf_weights.shape[3]
    fits = (
        shots == LANES
        and shots == 8 * devices
        and freq_total == trace_count * LANES
        and 2 * rank == LANES
        and 4 * rank == LANES * sub_count
        and traces % 2 == 0
        and trace_count % 2 == 0
    )
    chosen = fused_device if fits else general_device
    return chosen(seismic, band_low, band_high, leaf_weights, translations, level_table)


def solution(mesh):
    placed = (
        P(("groups", "trace", "space", "sub"), None, None),
        P("groups"),
        P("groups"),
        P(),
        P(),
        P(),
    )
    return jax.shard_map(
        per_device,
        mesh=mesh,
        in_specs=placed,
        out_specs=P(("groups", "trace", "space"), None, "sub", None),
        check_vma=False,
    )
```

```python
import functools
import math

import jax
import jax.numpy as jnp
import ml_dtypes
import numpy as np
from jax import lax
from jax.experimental import pallas as pl
from jax.experimental.pallas import tpu as pltpu
from jax.sharding import PartitionSpec as P

LANES = 128


def swapped(x, axis, distance):
    return lax.ppermute(x, axis, [(i, i ^ 1 << distance) for i in range(lax.axis_size(axis))])


def spectral_table(freq_total, samples):
    freq_range = jnp.arange(freq_total, dtype=jnp.int32)
    time_range = jnp.arange(samples, dtype=jnp.int32)
    phase = freq_range[:, None] * time_range[None, :] % samples
    angle = phase.astype(jnp.float32) * (2.0 * math.pi / samples)
    factor = 1.0 / math.sqrt(samples)
    return (jnp.concatenate([jnp.cos(angle), -jnp.sin(angle)], axis=0) * factor).astype(
        jnp.bfloat16
    )


def complex_product(left, right):
    highest = lax.Precision.HIGHEST
    real_part = jnp.dot(left[0], right[0], precision=highest) - jnp.dot(
        left[1], right[1], precision=highest
    )
    imag_part = jnp.dot(left[0], right[1], precision=highest) + jnp.dot(
        left[1], right[0], precision=highest
    )
    return jnp.stack([real_part, imag_part])


def swap_space(weights_now, bit_no):
    return swapped(weights_now, "space", bit_no)


def swap_trace(weights_now, bit_no):
    return swapped(weights_now, "trace", bit_no)


def merge_level(
    weights_now, partner, section_no, box_index, translations, level_table, sub_place, half_rank
):
    stride = 2**section_no
    upper_flag = box_index // stride % 2 == 1
    lower_part = jnp.where(upper_flag, partner, weights_now)
    upper_part = jnp.where(upper_flag, weights_now, partner)
    entries = lax.dynamic_index_in_dim(level_table[section_no], box_index, 0, keepdims=False)
    first_mat = lax.dynamic_index_in_dim(translations, entries[0], 0, keepdims=False)
    second_mat = lax.dynamic_index_in_dim(translations, entries[1], 0, keepdims=False)
    full_lower, full_upper = (
        lax.all_gather(lower_part, "sub", axis=1, tiled=True),
        lax.all_gather(upper_part, "sub", axis=1, tiled=True),
    )
    first_rows = lax.dynamic_slice_in_dim(first_mat, sub_place * half_rank, half_rank, 1)
    second_rows = lax.dynamic_slice_in_dim(second_mat, sub_place * half_rank, half_rank, 1)
    return complex_product(first_rows, full_lower) + complex_product(second_rows, full_upper)


def join_complex(parts):
    return jnp.stack([parts[:, 0, 0] - parts[:, 1, 1], parts[:, 0, 1] + parts[:, 1, 0]], axis=1)


def general_device(seismic, band_low, band_high, leaf_weights, translations, level_table):
    highest = lax.Precision.HIGHEST
    trace_count = lax.axis_size("trace")
    space_count = lax.axis_size("space")
    sub_count = lax.axis_size("sub")
    trace_place = lax.axis_index("trace")
    space_place = lax.axis_index("space")
    sub_place = lax.axis_index("sub")
    traces_here = seismic.shape[0]
    samples = seismic.shape[1]
    shots_count = seismic.shape[2]
    freq_total = leaf_weights.shape[1]
    rank_total = leaf_weights.shape[3]
    freq_block = freq_total // trace_count
    half_rank = rank_total // sub_count
    dft_rows = spectral_table(freq_total, samples)
    spectra = jnp.einsum(
        "kt,xts->xks", dft_rows, seismic, preferred_element_type=jnp.float32
    ).astype(jnp.bfloat16)
    spectra = spectra.reshape(traces_here, 2, freq_total, shots_count)
    freq_index = jnp.arange(freq_total, dtype=jnp.int32)
    band_mask = (
        (freq_index[:, None] >= band_low[None, :]) & (freq_index[:, None] < band_high[None, :])
    ).astype(jnp.bfloat16)
    masked = spectra * band_mask
    piece = masked.astype(jnp.float32)
    piece = piece.reshape(traces_here, 2, 1 * lax.axis_size("trace"), freq_block, shots_count)
    leaf_piece = leaf_weights.astype(jnp.float32)
    leaf_piece = leaf_piece.reshape(
        traces_here, 1 * lax.axis_size("trace"), freq_block, 2, rank_total
    )
    parts = jnp.einsum("iagfs,igfbr->gabrs", piece, leaf_piece, precision=highest)
    leaf_terms = lax.psum_scatter(join_complex(parts), "trace", scatter_dimension=0, tiled=True)[0]
    weights_now = lax.psum_scatter(leaf_terms, "sub", scatter_dimension=1, tiled=True)
    box_index = trace_place * space_count + space_place
    section_no = 0
    for bit_no in range(space_count.bit_length() - 1):
        partner = swap_space(weights_now, bit_no)
        weights_now = merge_level(
            weights_now,
            partner,
            section_no,
            box_index,
            translations,
            level_table,
            sub_place,
            half_rank,
        )
        section_no = section_no + 1
    for bit_no in range(trace_count.bit_length() - 1):
        partner = swap_trace(weights_now, bit_no)
        weights_now = merge_level(
            weights_now,
            partner,
            section_no,
            box_index,
            translations,
            level_table,
            sub_place,
            half_rank,
        )
        section_no = section_no + 1
    return weights_now[None]


def table_rows(freq_total, samples, chunks):
    phase = np.arange(freq_total)[:, None] * np.arange(samples)[None, :] % samples
    angle = phase.astype(np.float32) * np.float32(2.0 * math.pi / samples)
    factor = np.float32(1.0 / math.sqrt(samples))
    parts = np.stack([np.cos(angle), -np.sin(angle)]) * factor
    rows = parts.reshape(2, chunks, freq_total // chunks, samples).transpose(1, 0, 2, 3)
    return rows.reshape(chunks, 2 * freq_total // chunks, samples).astype(ml_dtypes.bfloat16)


def split_two(x):
    high = x.astype(jnp.bfloat16).astype(jnp.float32)
    return high, x - high


def fused_kernel(
    sizes,
    x_hbm,
    low_hbm,
    high_hbm,
    q_hbm,
    tab_hbm,
    tr_hbm,
    level_hbm,
    out_ref,
    band_v,
    level_ref,
    x_v,
    q_v,
    tab_v,
    tr_v,
    spec_v,
    mat_hi,
    mat_lo,
    send1,
    recv1,
    send2,
    recv2,
    load_sem,
    small_sem,
    send_sem1,
    recv_sem1,
    send_sem2,
    recv_sem2,
):
    trace_count, space_count, sub_count = sizes
    devices = trace_count * space_count * sub_count
    t, p, u = lax.axis_index("trace"), lax.axis_index("space"), lax.axis_index("sub")
    me = (t * space_count + p) * sub_count + u
    chunks = tab_v.shape[0]
    traces = q_v.shape[0]
    pairs = traces // 2
    bands = trace_count // chunks
    boxes = trace_count * space_count
    levels = mat_hi.shape[0]
    rank = tr_v.shape[2]
    half = rank // sub_count
    block = LANES // devices

    band_loads = [
        pltpu.make_async_copy(low_hbm, band_v.at[0], small_sem.at[0]),
        pltpu.make_async_copy(high_hbm, band_v.at[1], small_sem.at[1]),
    ]
    level_load = pltpu.make_async_copy(level_hbm, level_ref, small_sem.at[2])
    loads = []
    for h in range(chunks):
        loads.append(pltpu.make_async_copy(tab_hbm.at[h], tab_v.at[h], load_sem.at[len(loads)]))
    x_loads = []
    for j in range(traces):
        x_loads.append(
            pltpu.make_async_copy(
                x_hbm.at[j],
                x_v.at[j // 2, :, pl.ds(j % 2 * LANES, LANES)],
                load_sem.at[chunks + j],
            )
        )
    q_load = pltpu.make_async_copy(q_hbm, q_v, load_sem.at[chunks + traces])
    tr_load = pltpu.make_async_copy(tr_hbm, tr_v, load_sem.at[chunks + traces + 1])
    loads[0].start()
    for load in x_loads:
        load.start()
    for load in band_loads:
        load.start()
    q_load.start()
    for load in loads[1:]:
        load.start()
    level_load.start()
    tr_load.start()

    offsets = [
        (dt, dp, du)
        for dt in range(trace_count)
        for dp in range(space_count)
        for du in range(sub_count)
        if dt or dp or du
    ]
    offsets.sort(key=lambda o: -min(o[0], trace_count - o[0]) * 4 - o[1] * 2 - o[2])

    def place(offset):
        dt, dp, du = offset
        tt = lax.rem(t + dt, trace_count)
        pp = lax.rem(p + dp, space_count)
        uu = lax.rem(u + du, sub_count)
        return tt, pp, uu

    barrier = pltpu.get_barrier_semaphore()
    for offset in offsets:
        tt, pp, uu = place(offset)
        pl.semaphore_signal(
            barrier,
            inc=1,
            device_id={"trace": tt, "space": pp, "sub": uu},
            device_id_type=pl.DeviceIdType.MESH,
        )

    def place_matrices(level, q):
        stride = 2**level
        lower = [b for b in range(boxes) if b // stride % 2 == 0][q]
        for side in range(2):
            for child in range(2):
                entry = level_ref[level, child, lower + side * stride]
                real, imag = tr_v[entry, 0], tr_v[entry, 1]
                top = jnp.concatenate([real, -imag], axis=1)
                bottom = jnp.concatenate([imag, real], axis=1)
                columns = slice(child * LANES, (child + 1) * LANES)
                for part, rows in enumerate((top, bottom)):
                    high, rest = split_two(rows)
                    high, rest = high.astype(jnp.bfloat16), rest.astype(jnp.bfloat16)
                    if level < levels - 1:
                        at = side * 2 * rank + part * rank
                        mat_hi[level, q, at : at + rank, columns] = high
                        mat_lo[level, q, at : at + rank, columns] = rest
                    else:
                        for s in range(sub_count):
                            at = s * 4 * half + side * 2 * half + part * half
                            mine = slice(s * half, (s + 1) * half)
                            mat_hi[level, q, at : at + half, columns] = high[mine]
                            mat_lo[level, q, at : at + half, columns] = rest[mine]

    to_place = [(level, q) for level in range(levels) for q in range(boxes // 2)]
    per_pair = -(-len(to_place) // pairs)

    copies1 = []
    for h in range(chunks):
        loads[h].wait()
        if h == chunks - 1:
            level_load.wait()
            tr_load.wait()
        width = bands * LANES
        freq = lax.broadcasted_iota(jnp.int32, (width, LANES), 0) + h * width
        if h == 0:
            for load in band_loads:
                load.wait()
        keep = (freq >= band_v[0]) & (freq < band_v[1])
        for pair in range(pairs):
            if h == 0:
                x_loads[2 * pair].wait()
                x_loads[2 * pair + 1].wait()
            if h == chunks - 1:
                for level, q in to_place[pair * per_pair : (pair + 1) * per_pair]:
                    place_matrices(level, q)
            rows = jnp.dot(tab_v[h], x_v[pair], preferred_element_type=jnp.float32)
            for part in range(2):
                for k in range(2):
                    piece = rows[part * width : (part + 1) * width, k * LANES : (k + 1) * LANES]
                    piece = jnp.where(keep, piece, 0.0).astype(jnp.bfloat16)
                    j = 2 * pair + k
                    for g in range(bands):
                        spec_v[
                            h * bands + g,
                            j * LANES : (j + 1) * LANES,
                            part * LANES : (part + 1) * LANES,
                        ] = piece[g * LANES : (g + 1) * LANES]
        if h == 0:
            q_load.wait()
        leaves = []
        for g in range(h * bands, (h + 1) * bands):
            left = jnp.concatenate(
                [q_v[j, :, g * LANES : (g + 1) * LANES] for j in range(traces)], axis=1
            )
            both = jnp.dot(left, spec_v[g], preferred_element_type=jnp.float32)
            real = both[:rank, :LANES] - both[rank:, LANES:]
            imag = both[rank:, :LANES] + both[:rank, LANES:]
            turned = jnp.concatenate([real, imag], axis=0).T
            leaves.append(turned.reshape(devices, block, LANES))
        send1[h] = jnp.concatenate(leaves, axis=1).astype(jnp.bfloat16)
        if h == 0:
            pl.semaphore_wait(barrier, devices - 1)
        for i, offset in enumerate(offsets):
            tt, pp, uu = place(offset)
            copy = pltpu.make_async_remote_copy(
                src_ref=send1.at[h, (tt * space_count + pp) * sub_count + uu],
                dst_ref=recv1.at[h, i],
                send_sem=send_sem1.at[h, i],
                recv_sem=recv_sem1.at[h, i],
                device_id={"trace": tt, "space": pp, "sub": uu},
                device_id_type=pl.DeviceIdType.MESH,
            )
            copy.start()
            copies1.append(copy)

    same = [send1[h, me].astype(jnp.float32) for h in range(chunks)]
    other = [None] * chunks
    for h in range(chunks):
        for i, offset in enumerate(offsets):
            copies1[h * len(offsets) + i].wait_recv()
            got = recv1[h, i].astype(jnp.float32)
            if offset[1] == 0:
                same[h] = same[h] + got
            else:
                other[h] = got if other[h] is None else other[h] + got
    first = p == 0
    now = [None] * boxes
    for h in range(chunks):
        for place_no in range(space_count):
            total = jnp.where(first == (place_no == 0), same[h], other[h])
            for g in range(bands):
                box = (h * bands + g) * space_count + place_no
                now[box] = total[g * block : (g + 1) * block]

    for level in range(levels):
        stride = 2**level
        lowers = [b for b in range(boxes) if b // stride % 2 == 0]
        for q, lower in enumerate(lowers):
            both = jnp.concatenate([now[lower], now[lower + stride]], axis=1)
            left = jnp.concatenate(split_two(both), axis=0).astype(jnp.bfloat16)
            dims = (((1,), (1,)), ((), ()))
            main = lax.dot_general(
                left, mat_hi[level, q], dims, preferred_element_type=jnp.float32
            )
            rest = lax.dot_general(
                left, mat_lo[level, q], dims, preferred_element_type=jnp.float32
            )
            joined = main[:block] + (main[block:] + rest[:block])
            if level < levels - 1:
                now[lower], now[lower + stride] = joined[:, :LANES], joined[:, LANES:]
            else:
                for s in range(sub_count):
                    for side in range(2):
                        at = s * LANES + side * 2 * half
                        mine = joined[:, at : at + 2 * half]
                        send2[(q + side * len(lowers)) * sub_count + s] = jnp.concatenate(
                            [mine[: block // 2], mine[block // 2 :]], axis=1
                        )

    copies2 = []
    for i, offset in enumerate(offsets):
        tt, pp, uu = place(offset)
        copy = pltpu.make_async_remote_copy(
            src_ref=send2.at[(tt * space_count + pp) * sub_count + uu],
            dst_ref=recv2.at[me],
            send_sem=send_sem2.at[i],
            recv_sem=recv_sem2.at[i],
            device_id={"trace": tt, "space": pp, "sub": uu},
            device_id_type=pl.DeviceIdType.MESH,
        )
        copy.start()
        copies2.append(copy)
    recv2[me] = send2[me]
    for copy in copies2:
        copy.wait_recv()
    pieces = []
    for d in range(devices):
        got = recv2[d]
        pieces += [got[:, : 2 * half], got[:, 2 * half :]]
    out_ref[...] = jnp.concatenate(pieces, axis=0).T.reshape(1, 2, half, LANES)
    for copy in copies1 + copies2:
        copy.wait_send()


def fused_device(seismic, band_low, band_high, leaf_weights, translations, level_table):
    sizes = tuple(lax.axis_size(name) for name in ("trace", "space", "sub"))
    devices = math.prod(sizes)
    boxes = sizes[0] * sizes[1]
    traces, samples, shots = seismic.shape
    freq_total, rank = leaf_weights.shape[1], leaf_weights.shape[3]
    chunks = 2
    levels = level_table.shape[0]
    table = jnp.asarray(table_rows(freq_total, samples, chunks))
    weights = leaf_weights.transpose(0, 2, 3, 1).reshape(traces, 2 * rank, freq_total)
    block = shots // devices
    rows = sizes[0] // chunks * block
    hbm_spec = pl.BlockSpec(memory_space=pltpu.HBM)
    vmem_spec = pl.BlockSpec(memory_space=pltpu.VMEM)
    dma = pltpu.SemaphoreType.DMA
    return pl.pallas_call(
        functools.partial(fused_kernel, sizes),
        out_shape=jax.ShapeDtypeStruct((1, 2, rank // sizes[2], shots), jnp.float32),
        in_specs=[hbm_spec] * 7,
        out_specs=vmem_spec,
        scratch_shapes=[
            pltpu.VMEM((2, 1, shots), jnp.int32),
            pltpu.SMEM((levels, 2, boxes), jnp.int32),
            pltpu.VMEM((traces // 2, samples, 2 * shots), jnp.bfloat16),
            pltpu.VMEM(weights.shape, jnp.bfloat16),
            pltpu.VMEM(table.shape, jnp.bfloat16),
            pltpu.VMEM(translations.shape, jnp.float32),
            pltpu.VMEM((sizes[0], traces * LANES, 2 * LANES), jnp.bfloat16),
            pltpu.VMEM((levels, boxes // 2, 4 * rank, 4 * rank), jnp.bfloat16),
            pltpu.VMEM((levels, boxes // 2, 4 * rank, 4 * rank), jnp.bfloat16),
            pltpu.VMEM((chunks, devices, rows, LANES), jnp.bfloat16),
            pltpu.VMEM((chunks, devices - 1, rows, LANES), jnp.bfloat16),
            pltpu.VMEM((devices, block // 2, LANES), jnp.float32),
            pltpu.VMEM((devices, block // 2, LANES), jnp.float32),
            dma((chunks + traces + 2,)),
            dma((3,)),
            dma((chunks, devices - 1)),
            dma((chunks, devices - 1)),
            dma((devices - 1,)),
            dma((devices - 1,)),
        ],
        compiler_params=pltpu.CompilerParams(
            collective_id=0, has_side_effects=True, vmem_limit_bytes=56 * 2**20
        ),
    )(
        seismic,
        band_low.reshape(1, shots),
        band_high.reshape(1, shots),
        weights,
        table,
        translations,
        level_table.transpose(0, 2, 1),
    )


def per_device(seismic, band_low, band_high, leaf_weights, translations, level_table):
    trace_count, space_count, sub_count = (
        lax.axis_size(name) for name in ("trace", "space", "sub")
    )
    devices = trace_count * space_count * sub_count
    traces, _, shots = seismic.shape
    freq_total, rank = leaf_weights.shape[1], leaf_weights.shape[3]
    fits = (
        shots == LANES
        and shots == 8 * devices
        and freq_total == trace_count * LANES
        and 2 * rank == LANES
        and 4 * rank == LANES * sub_count
        and traces % 2 == 0
        and trace_count % 2 == 0
    )
    chosen = fused_device if fits else general_device
    return chosen(seismic, band_low, band_high, leaf_weights, translations, level_table)


def solution(mesh):
    placed = (
        P(("groups", "trace", "space", "sub"), None, None),
        P("groups"),
        P("groups"),
        P(),
        P(),
        P(),
    )
    return jax.shard_map(
        per_device,
        mesh=mesh,
        in_specs=placed,
        out_specs=P(("groups", "trace", "space"), None, "sub", None),
        check_vma=False,
    )
```

```python
import functools
import math

import jax
import jax.numpy as jnp
import ml_dtypes
import numpy as np
from jax import lax
from jax.experimental import pallas as pl
from jax.experimental.pallas import tpu as pltpu
from jax.sharding import PartitionSpec as P

LANES = 128


def swapped(x, axis, distance):
    return lax.ppermute(x, axis, [(i, i ^ 1 << distance) for i in range(lax.axis_size(axis))])


def spectral_table(freq_total, samples):
    freq_range = jnp.arange(freq_total, dtype=jnp.int32)
    time_range = jnp.arange(samples, dtype=jnp.int32)
    phase = freq_range[:, None] * time_range[None, :] % samples
    angle = phase.astype(jnp.float32) * (2.0 * math.pi / samples)
    factor = 1.0 / math.sqrt(samples)
    return (jnp.concatenate([jnp.cos(angle), -jnp.sin(angle)], axis=0) * factor).astype(
        jnp.bfloat16
    )


def complex_product(left, right):
    highest = lax.Precision.HIGHEST
    real_part = jnp.dot(left[0], right[0], precision=highest) - jnp.dot(
        left[1], right[1], precision=highest
    )
    imag_part = jnp.dot(left[0], right[1], precision=highest) + jnp.dot(
        left[1], right[0], precision=highest
    )
    return jnp.stack([real_part, imag_part])


def swap_space(weights_now, bit_no):
    return swapped(weights_now, "space", bit_no)


def swap_trace(weights_now, bit_no):
    return swapped(weights_now, "trace", bit_no)


def merge_level(
    weights_now, partner, section_no, box_index, translations, level_table, sub_place, half_rank
):
    stride = 2**section_no
    upper_flag = box_index // stride % 2 == 1
    lower_part = jnp.where(upper_flag, partner, weights_now)
    upper_part = jnp.where(upper_flag, weights_now, partner)
    entries = lax.dynamic_index_in_dim(level_table[section_no], box_index, 0, keepdims=False)
    first_mat = lax.dynamic_index_in_dim(translations, entries[0], 0, keepdims=False)
    second_mat = lax.dynamic_index_in_dim(translations, entries[1], 0, keepdims=False)
    full_lower, full_upper = (
        lax.all_gather(lower_part, "sub", axis=1, tiled=True),
        lax.all_gather(upper_part, "sub", axis=1, tiled=True),
    )
    first_rows = lax.dynamic_slice_in_dim(first_mat, sub_place * half_rank, half_rank, 1)
    second_rows = lax.dynamic_slice_in_dim(second_mat, sub_place * half_rank, half_rank, 1)
    return complex_product(first_rows, full_lower) + complex_product(second_rows, full_upper)


def join_complex(parts):
    return jnp.stack([parts[:, 0, 0] - parts[:, 1, 1], parts[:, 0, 1] + parts[:, 1, 0]], axis=1)


def general_device(seismic, band_low, band_high, leaf_weights, translations, level_table):
    highest = lax.Precision.HIGHEST
    trace_count = lax.axis_size("trace")
    space_count = lax.axis_size("space")
    sub_count = lax.axis_size("sub")
    trace_place = lax.axis_index("trace")
    space_place = lax.axis_index("space")
    sub_place = lax.axis_index("sub")
    traces_here = seismic.shape[0]
    samples = seismic.shape[1]
    shots_count = seismic.shape[2]
    freq_total = leaf_weights.shape[1]
    rank_total = leaf_weights.shape[3]
    freq_block = freq_total // trace_count
    half_rank = rank_total // sub_count
    dft_rows = spectral_table(freq_total, samples)
    spectra = jnp.einsum(
        "kt,xts->xks", dft_rows, seismic, preferred_element_type=jnp.float32
    ).astype(jnp.bfloat16)
    spectra = spectra.reshape(traces_here, 2, freq_total, shots_count)
    freq_index = jnp.arange(freq_total, dtype=jnp.int32)
    band_mask = (
        (freq_index[:, None] >= band_low[None, :]) & (freq_index[:, None] < band_high[None, :])
    ).astype(jnp.bfloat16)
    masked = spectra * band_mask
    piece = masked.astype(jnp.float32)
    piece = piece.reshape(traces_here, 2, 1 * lax.axis_size("trace"), freq_block, shots_count)
    leaf_piece = leaf_weights.astype(jnp.float32)
    leaf_piece = leaf_piece.reshape(
        traces_here, 1 * lax.axis_size("trace"), freq_block, 2, rank_total
    )
    parts = jnp.einsum("iagfs,igfbr->gabrs", piece, leaf_piece, precision=highest)
    leaf_terms = lax.psum_scatter(join_complex(parts), "trace", scatter_dimension=0, tiled=True)[0]
    weights_now = lax.psum_scatter(leaf_terms, "sub", scatter_dimension=1, tiled=True)
    box_index = trace_place * space_count + space_place
    section_no = 0
    for bit_no in range(space_count.bit_length() - 1):
        partner = swap_space(weights_now, bit_no)
        weights_now = merge_level(
            weights_now,
            partner,
            section_no,
            box_index,
            translations,
            level_table,
            sub_place,
            half_rank,
        )
        section_no = section_no + 1
    for bit_no in range(trace_count.bit_length() - 1):
        partner = swap_trace(weights_now, bit_no)
        weights_now = merge_level(
            weights_now,
            partner,
            section_no,
            box_index,
            translations,
            level_table,
            sub_place,
            half_rank,
        )
        section_no = section_no + 1
    return weights_now[None]


def table_rows(freq_total, samples, chunks):
    phase = np.arange(freq_total)[:, None] * np.arange(samples)[None, :] % samples
    angle = phase.astype(np.float32) * np.float32(2.0 * math.pi / samples)
    factor = np.float32(1.0 / math.sqrt(samples))
    parts = np.stack([np.cos(angle), -np.sin(angle)]) * factor
    rows = parts.reshape(2, chunks, freq_total // chunks, samples).transpose(1, 0, 2, 3)
    return rows.reshape(chunks, 2 * freq_total // chunks, samples).astype(ml_dtypes.bfloat16)


def split_two(x):
    high = x.astype(jnp.bfloat16).astype(jnp.float32)
    return high, x - high


def fused_kernel(
    sizes,
    x_hbm,
    low_hbm,
    high_hbm,
    q_hbm,
    tab_hbm,
    tr_hbm,
    level_hbm,
    out_ref,
    band_v,
    level_ref,
    x_v,
    q_v,
    tab_v,
    tr_v,
    spec_v,
    mat_hi,
    mat_lo,
    stage,
    send1,
    recv1,
    send2,
    recv2,
    load_sem,
    small_sem,
    send_sem1,
    recv_sem1,
    send_sem2,
    recv_sem2,
):
    trace_count, space_count, sub_count = sizes
    devices = trace_count * space_count * sub_count
    t, p, u = lax.axis_index("trace"), lax.axis_index("space"), lax.axis_index("sub")
    me = (t * space_count + p) * sub_count + u
    chunks = tab_v.shape[0]
    traces = q_v.shape[0]
    pairs = traces // 2
    bands = trace_count // chunks
    boxes = trace_count * space_count
    levels = mat_hi.shape[0]
    rank = tr_v.shape[2]
    half = rank // sub_count
    block = LANES // devices

    band_loads = [
        pltpu.make_async_copy(low_hbm, band_v.at[0], small_sem.at[0]),
        pltpu.make_async_copy(high_hbm, band_v.at[1], small_sem.at[1]),
    ]
    level_load = pltpu.make_async_copy(level_hbm, level_ref, small_sem.at[2])
    loads = []
    for h in range(chunks):
        loads.append(pltpu.make_async_copy(tab_hbm.at[h], tab_v.at[h], load_sem.at[len(loads)]))

    def x_load(pair, k):
        return pltpu.make_async_copy(
            x_hbm.at[2 * pair + k],
            x_v.at[pair, :, pl.ds(k * LANES, LANES)],
            load_sem.at[chunks + 2 * pair + k],
        )

    q_load = pltpu.make_async_copy(q_hbm, q_v, load_sem.at[chunks + traces])
    tr_load = pltpu.make_async_copy(tr_hbm, tr_v, load_sem.at[chunks + traces + 1])
    loads[0].start()
    for j in range(traces):
        x_load(j // 2, j % 2).start()
    for load in band_loads:
        load.start()
    q_load.start()
    for load in loads[1:]:
        load.start()
    level_load.start()
    tr_load.start()

    def place(i):
        tt = lax.rem(t + i // (space_count * sub_count), trace_count)
        pp = lax.rem(p + i // sub_count % space_count, space_count)
        uu = lax.rem(u + i % sub_count, sub_count)
        return (tt * space_count + pp) * sub_count + uu, {"trace": tt, "space": pp, "sub": uu}

    barrier = pltpu.get_barrier_semaphore()

    @pl.loop(1, devices)
    def _(i):
        _, target = place(i)
        pl.semaphore_signal(
            barrier, inc=1, device_id=target, device_id_type=pl.DeviceIdType.MESH
        )

    def place_matrices(level, q):
        stride = 2**level
        lower = q // stride * (2 * stride) + q % stride
        for side in range(2):
            for child in range(2):
                entry = level_ref[level, child, lower + side * stride]
                real, imag = tr_v[entry, 0], tr_v[entry, 1]
                top = jnp.concatenate([real, -imag], axis=1)
                bottom = jnp.concatenate([imag, real], axis=1)
                columns = slice(child * LANES, (child + 1) * LANES)
                for part, rows in enumerate((top, bottom)):
                    high, rest = split_two(rows)
                    high, rest = high.astype(jnp.bfloat16), rest.astype(jnp.bfloat16)
                    if level < levels - 1:
                        at = side * 2 * rank + part * rank
                        mat_hi[level, q, at : at + rank, columns] = high
                        mat_lo[level, q, at : at + rank, columns] = rest
                    else:
                        for s in range(sub_count):
                            at = s * 4 * half + side * 2 * half + part * half
                            mine = slice(s * half, (s + 1) * half)
                            mat_hi[level, q, at : at + half, columns] = high[mine]
                            mat_lo[level, q, at : at + half, columns] = rest[mine]

    def copy1(h, i):
        d, target = place(i)
        return pltpu.make_async_remote_copy(
            src_ref=send1.at[h, d],
            dst_ref=recv1.at[h, i],
            send_sem=send_sem1.at[h, i],
            recv_sem=recv_sem1.at[h, i],
            device_id=target,
            device_id_type=pl.DeviceIdType.MESH,
        )

    def copy2(i):
        d, target = place(i)
        return pltpu.make_async_remote_copy(
            src_ref=send2.at[d],
            dst_ref=recv2.at[me],
            send_sem=send_sem2.at[i],
            recv_sem=recv_sem2.at[i],
            device_id=target,
            device_id_type=pl.DeviceIdType.MESH,
        )

    width = bands * LANES
    for h in range(chunks):
        loads[h].wait()
        if h == 0:
            for load in band_loads:
                load.wait()
        if h == chunks - 1:
            level_load.wait()
            tr_load.wait()

        @pl.loop(0, pairs)
        def _(pair, h=h):
            if h == 0:
                for k in range(2):
                    x_load(pair, k).wait()
            if h == chunks - 1:
                for level in range(levels):
                    place_matrices(level, pair)
            rows = jnp.dot(tab_v[h], x_v[pair], preferred_element_type=jnp.float32)
            freq = lax.broadcasted_iota(jnp.int32, (width, LANES), 0) + h * width
            keep = (freq >= band_v[0]) & (freq < band_v[1])
            for part in range(2):
                for k in range(2):
                    piece = rows[part * width : (part + 1) * width, k * LANES : (k + 1) * LANES]
                    piece = jnp.where(keep, piece, 0.0).astype(jnp.bfloat16)
                    for g in range(bands):
                        columns = slice(part * LANES, (part + 1) * LANES)
                        spec_v[h * bands + g, 2 * pair + k, :, columns] = piece[
                            g * LANES : (g + 1) * LANES
                        ]

        if h == 0:
            q_load.wait()

        @pl.loop(0, bands)
        def _(g, h=h):
            band = h * bands + g
            at = pl.ds(pl.multiple_of(band * LANES, LANES), LANES)
            left = jnp.concatenate([q_v[j, :, at] for j in range(traces)], axis=1)
            right = spec_v[band].reshape(traces * LANES, 2 * LANES)
            both = jnp.dot(left, right, preferred_element_type=jnp.float32)
            real = both[:rank, :LANES] - both[rank:, LANES:]
            imag = both[rank:, :LANES] + both[:rank, LANES:]
            turned = jnp.concatenate([real, imag], axis=0).T
            stage[:, pl.ds(pl.multiple_of(g * block, block), block), :] = turned.reshape(
                devices, block, LANES
            )

        send1[h] = stage[...].astype(jnp.bfloat16)
        if h == 0:
            pl.semaphore_wait(barrier, devices - 1)

        @pl.loop(1, devices)
        def _(i, h=h):
            copy1(h, i).start()

    def arrived(n, totals, dp):
        i = n // sub_count * (space_count * sub_count) + dp * sub_count + n % sub_count
        for h in range(chunks):
            copy1(h, i).wait_recv()
        return tuple(totals[h] + recv1[h, i].astype(jnp.float32) for h in range(chunks))

    same = tuple(send1[h, me].astype(jnp.float32) for h in range(chunks))
    same = lax.fori_loop(1, trace_count * sub_count, functools.partial(arrived, dp=0), same)
    other = tuple(jnp.zeros_like(part) for part in same)
    other = lax.fori_loop(0, trace_count * sub_count, functools.partial(arrived, dp=1), other)
    first = p == 0
    now = [None] * boxes
    for h in range(chunks):
        for place_no in range(space_count):
            total = jnp.where(first == (place_no == 0), same[h], other[h])
            for g in range(bands):
                box = (h * bands + g) * space_count + place_no
                now[box] = total[g * block : (g + 1) * block]

    for level in range(levels):
        stride = 2**level
        lowers = [b for b in range(boxes) if b // stride % 2 == 0]
        for q, lower in enumerate(lowers):
            both = jnp.concatenate([now[lower], now[lower + stride]], axis=1)
            left = jnp.concatenate(split_two(both), axis=0).astype(jnp.bfloat16)
            dims = (((1,), (1,)), ((), ()))
            main = lax.dot_general(
                left, mat_hi[level, q], dims, preferred_element_type=jnp.float32
            )
            rest = lax.dot_general(
                left, mat_lo[level, q], dims, preferred_element_type=jnp.float32
            )
            joined = main[:block] + (main[block:] + rest[:block])
            if level < levels - 1:
                now[lower], now[lower + stride] = joined[:, :LANES], joined[:, LANES:]
            else:
                for s in range(sub_count):
                    for side in range(2):
                        at = s * LANES + side * 2 * half
                        mine = joined[:, at : at + 2 * half]
                        send2[(q + side * len(lowers)) * sub_count + s] = jnp.concatenate(
                            [mine[: block // 2], mine[block // 2 :]], axis=1
                        )

    @pl.loop(1, devices)
    def _(i):
        copy2(i).start()

    recv2[me] = send2[me]

    @pl.loop(1, devices)
    def _(i):
        copy2(i).wait_recv()

    pieces = []
    for d in range(devices):
        got = recv2[d]
        pieces += [got[:, : 2 * half], got[:, 2 * half :]]
    out_ref[...] = jnp.concatenate(pieces, axis=0).T.reshape(1, 2, half, LANES)

    @pl.loop(1, devices)
    def _(i):
        for h in range(chunks):
            copy1(h, i).wait_send()
        copy2(i).wait_send()


def fused_device(seismic, band_low, band_high, leaf_weights, translations, level_table):
    sizes = tuple(lax.axis_size(name) for name in ("trace", "space", "sub"))
    devices = math.prod(sizes)
    boxes = sizes[0] * sizes[1]
    traces, samples, shots = seismic.shape
    freq_total, rank = leaf_weights.shape[1], leaf_weights.shape[3]
    chunks = 2
    levels = level_table.shape[0]
    table = jnp.asarray(table_rows(freq_total, samples, chunks))
    weights = leaf_weights.transpose(0, 2, 3, 1).reshape(traces, 2 * rank, freq_total)
    block = shots // devices
    rows = sizes[0] // chunks * block
    hbm_spec = pl.BlockSpec(memory_space=pltpu.HBM)
    vmem_spec = pl.BlockSpec(memory_space=pltpu.VMEM)
    dma = pltpu.SemaphoreType.DMA
    return pl.pallas_call(
        functools.partial(fused_kernel, sizes),
        out_shape=jax.ShapeDtypeStruct((1, 2, rank // sizes[2], shots), jnp.float32),
        in_specs=[hbm_spec] * 7,
        out_specs=vmem_spec,
        scratch_shapes=[
            pltpu.VMEM((2, 1, shots), jnp.int32),
            pltpu.SMEM((levels, 2, boxes), jnp.int32),
            pltpu.VMEM((traces // 2, samples, 2 * shots), jnp.bfloat16),
            pltpu.VMEM(weights.shape, jnp.bfloat16),
            pltpu.VMEM(table.shape, jnp.bfloat16),
            pltpu.VMEM(translations.shape, jnp.float32),
            pltpu.VMEM((sizes[0], traces, LANES, 2 * LANES), jnp.bfloat16),
            pltpu.VMEM((levels, boxes // 2, 4 * rank, 4 * rank), jnp.bfloat16),
            pltpu.VMEM((levels, boxes // 2, 4 * rank, 4 * rank), jnp.bfloat16),
            pltpu.VMEM((devices, rows, LANES), jnp.float32),
            pltpu.VMEM((chunks, devices, rows, LANES), jnp.bfloat16),
            pltpu.VMEM((chunks, devices, rows, LANES), jnp.bfloat16),
            pltpu.VMEM((devices, block // 2, LANES), jnp.float32),
            pltpu.VMEM((devices, block // 2, LANES), jnp.float32),
            dma((chunks + traces + 2,)),
            dma((3,)),
            dma((chunks, devices)),
            dma((chunks, devices)),
            dma((devices,)),
            dma((devices,)),
        ],
        compiler_params=pltpu.CompilerParams(
            collective_id=0, has_side_effects=True, vmem_limit_bytes=56 * 2**20
        ),
    )(
        seismic,
        band_low.reshape(1, shots),
        band_high.reshape(1, shots),
        weights,
        table,
        translations,
        level_table.transpose(0, 2, 1),
    )


def per_device(seismic, band_low, band_high, leaf_weights, translations, level_table):
    trace_count, space_count, sub_count = (
        lax.axis_size(name) for name in ("trace", "space", "sub")
    )
    devices = trace_count * space_count * sub_count
    traces, _, shots = seismic.shape
    freq_total, rank = leaf_weights.shape[1], leaf_weights.shape[3]
    fits = (
        shots == LANES
        and shots == 8 * devices
        and freq_total == trace_count * LANES
        and 2 * rank == LANES
        and 4 * rank == LANES * sub_count
        and traces % 2 == 0
        and space_count == 2
        and trace_count % 2 == 0
    )
    chosen = fused_device if fits else general_device
    return chosen(seismic, band_low, band_high, leaf_weights, translations, level_table)


def solution(mesh):
    placed = (
        P(("groups", "trace", "space", "sub"), None, None),
        P("groups"),
        P("groups"),
        P(),
        P(),
        P(),
    )
    return jax.shard_map(
        per_device,
        mesh=mesh,
        in_specs=placed,
        out_specs=P(("groups", "trace", "space"), None, "sub", None),
        check_vma=False,
    )
```

```python
import functools
import math

import jax
import jax.numpy as jnp
import ml_dtypes
import numpy as np
from jax import lax
from jax.experimental import pallas as pl
from jax.experimental.pallas import tpu as pltpu
from jax.sharding import PartitionSpec as P

LANES = 128


def swapped(x, axis, distance):
    return lax.ppermute(x, axis, [(i, i ^ 1 << distance) for i in range(lax.axis_size(axis))])


def spectral_table(freq_total, samples):
    freq_range = jnp.arange(freq_total, dtype=jnp.int32)
    time_range = jnp.arange(samples, dtype=jnp.int32)
    phase = freq_range[:, None] * time_range[None, :] % samples
    angle = phase.astype(jnp.float32) * (2.0 * math.pi / samples)
    factor = 1.0 / math.sqrt(samples)
    return (jnp.concatenate([jnp.cos(angle), -jnp.sin(angle)], axis=0) * factor).astype(
        jnp.bfloat16
    )


def complex_product(left, right):
    highest = lax.Precision.HIGHEST
    real_part = jnp.dot(left[0], right[0], precision=highest) - jnp.dot(
        left[1], right[1], precision=highest
    )
    imag_part = jnp.dot(left[0], right[1], precision=highest) + jnp.dot(
        left[1], right[0], precision=highest
    )
    return jnp.stack([real_part, imag_part])


def swap_space(weights_now, bit_no):
    return swapped(weights_now, "space", bit_no)


def swap_trace(weights_now, bit_no):
    return swapped(weights_now, "trace", bit_no)


def merge_level(
    weights_now, partner, section_no, box_index, translations, level_table, sub_place, half_rank
):
    stride = 2**section_no
    upper_flag = box_index // stride % 2 == 1
    lower_part = jnp.where(upper_flag, partner, weights_now)
    upper_part = jnp.where(upper_flag, weights_now, partner)
    entries = lax.dynamic_index_in_dim(level_table[section_no], box_index, 0, keepdims=False)
    first_mat = lax.dynamic_index_in_dim(translations, entries[0], 0, keepdims=False)
    second_mat = lax.dynamic_index_in_dim(translations, entries[1], 0, keepdims=False)
    full_lower, full_upper = (
        lax.all_gather(lower_part, "sub", axis=1, tiled=True),
        lax.all_gather(upper_part, "sub", axis=1, tiled=True),
    )
    first_rows = lax.dynamic_slice_in_dim(first_mat, sub_place * half_rank, half_rank, 1)
    second_rows = lax.dynamic_slice_in_dim(second_mat, sub_place * half_rank, half_rank, 1)
    return complex_product(first_rows, full_lower) + complex_product(second_rows, full_upper)


def join_complex(parts):
    return jnp.stack([parts[:, 0, 0] - parts[:, 1, 1], parts[:, 0, 1] + parts[:, 1, 0]], axis=1)


def general_device(seismic, band_low, band_high, leaf_weights, translations, level_table):
    highest = lax.Precision.HIGHEST
    trace_count = lax.axis_size("trace")
    space_count = lax.axis_size("space")
    sub_count = lax.axis_size("sub")
    trace_place = lax.axis_index("trace")
    space_place = lax.axis_index("space")
    sub_place = lax.axis_index("sub")
    traces_here = seismic.shape[0]
    samples = seismic.shape[1]
    shots_count = seismic.shape[2]
    freq_total = leaf_weights.shape[1]
    rank_total = leaf_weights.shape[3]
    freq_block = freq_total // trace_count
    half_rank = rank_total // sub_count
    dft_rows = spectral_table(freq_total, samples)
    spectra = jnp.einsum(
        "kt,xts->xks", dft_rows, seismic, preferred_element_type=jnp.float32
    ).astype(jnp.bfloat16)
    spectra = spectra.reshape(traces_here, 2, freq_total, shots_count)
    freq_index = jnp.arange(freq_total, dtype=jnp.int32)
    band_mask = (
        (freq_index[:, None] >= band_low[None, :]) & (freq_index[:, None] < band_high[None, :])
    ).astype(jnp.bfloat16)
    masked = spectra * band_mask
    piece = masked.astype(jnp.float32)
    piece = piece.reshape(traces_here, 2, 1 * lax.axis_size("trace"), freq_block, shots_count)
    leaf_piece = leaf_weights.astype(jnp.float32)
    leaf_piece = leaf_piece.reshape(
        traces_here, 1 * lax.axis_size("trace"), freq_block, 2, rank_total
    )
    parts = jnp.einsum("iagfs,igfbr->gabrs", piece, leaf_piece, precision=highest)
    leaf_terms = lax.psum_scatter(join_complex(parts), "trace", scatter_dimension=0, tiled=True)[0]
    weights_now = lax.psum_scatter(leaf_terms, "sub", scatter_dimension=1, tiled=True)
    box_index = trace_place * space_count + space_place
    section_no = 0
    for bit_no in range(space_count.bit_length() - 1):
        partner = swap_space(weights_now, bit_no)
        weights_now = merge_level(
            weights_now,
            partner,
            section_no,
            box_index,
            translations,
            level_table,
            sub_place,
            half_rank,
        )
        section_no = section_no + 1
    for bit_no in range(trace_count.bit_length() - 1):
        partner = swap_trace(weights_now, bit_no)
        weights_now = merge_level(
            weights_now,
            partner,
            section_no,
            box_index,
            translations,
            level_table,
            sub_place,
            half_rank,
        )
        section_no = section_no + 1
    return weights_now[None]


def table_rows(freq_total, samples, chunks):
    phase = np.arange(freq_total)[:, None] * np.arange(samples)[None, :] % samples
    angle = phase.astype(np.float32) * np.float32(2.0 * math.pi / samples)
    factor = np.float32(1.0 / math.sqrt(samples))
    parts = np.stack([np.cos(angle), -np.sin(angle)]) * factor
    rows = parts.reshape(2, chunks, freq_total // chunks, samples).transpose(1, 0, 2, 3)
    return rows.reshape(chunks, 2 * freq_total // chunks, samples).astype(ml_dtypes.bfloat16)


def split_two(x):
    high = x.astype(jnp.bfloat16).astype(jnp.float32)
    return high, x - high


def fused_kernel(
    sizes,
    x_hbm,
    low_hbm,
    high_hbm,
    q_hbm,
    tab_hbm,
    tr_hbm,
    level_hbm,
    out_ref,
    band_v,
    level_ref,
    x_v,
    q_v,
    tab_v,
    tr_v,
    spec_v,
    mat_hi,
    mat_lo,
    send,
    recv,
    load_sem,
    small_sem,
    send_sem,
    recv_sem,
):
    trace_count, space_count, sub_count = sizes
    devices = trace_count * space_count * sub_count
    t, p, u = lax.axis_index("trace"), lax.axis_index("space"), lax.axis_index("sub")
    me = (t * space_count + p) * sub_count + u
    chunks = tab_v.shape[0]
    traces = q_v.shape[0]
    pairs = traces // 2
    bands = trace_count // chunks
    boxes = trace_count * space_count
    levels = mat_hi.shape[0]
    rank = tr_v.shape[2]
    half = rank // sub_count

    band_loads = [
        pltpu.make_async_copy(low_hbm, band_v.at[0], small_sem.at[0]),
        pltpu.make_async_copy(high_hbm, band_v.at[1], small_sem.at[1]),
    ]
    level_load = pltpu.make_async_copy(level_hbm, level_ref, small_sem.at[2])
    loads = []
    for h in range(chunks):
        loads.append(pltpu.make_async_copy(tab_hbm.at[h], tab_v.at[h], load_sem.at[len(loads)]))
    x_loads = []
    for j in range(traces):
        x_loads.append(
            pltpu.make_async_copy(
                x_hbm.at[j],
                x_v.at[j // 2, :, pl.ds(j % 2 * LANES, LANES)],
                load_sem.at[chunks + j],
            )
        )
    q_load = pltpu.make_async_copy(q_hbm, q_v, load_sem.at[chunks + traces])
    tr_load = pltpu.make_async_copy(tr_hbm, tr_v, load_sem.at[chunks + traces + 1])
    loads[0].start()
    for load in x_loads:
        load.start()
    for load in band_loads:
        load.start()
    q_load.start()
    for load in loads[1:]:
        load.start()
    level_load.start()
    tr_load.start()

    offsets = [
        (dt, dp, du)
        for dt in range(trace_count)
        for dp in range(space_count)
        for du in range(sub_count)
        if dt or dp or du
    ]
    offsets.sort(key=lambda o: -min(o[0], trace_count - o[0]) * 4 - o[1] * 2 - o[2])

    def place(offset):
        dt, dp, du = offset
        tt = lax.rem(t + dt, trace_count)
        pp = lax.rem(p + dp, space_count)
        uu = lax.rem(u + du, sub_count)
        return tt, pp, uu

    barrier = pltpu.get_barrier_semaphore()
    for offset in offsets:
        tt, pp, uu = place(offset)
        pl.semaphore_signal(
            barrier,
            inc=1,
            device_id={"trace": tt, "space": pp, "sub": uu},
            device_id_type=pl.DeviceIdType.MESH,
        )

    def place_matrices(level, q):
        stride = 2**level
        lower = [b for b in range(boxes) if b // stride % 2 == 0][q]
        for side in range(2):
            for child in range(2 if level else 1):
                entry = level_ref[level, child if level else p, lower + side * stride]
                real, imag = tr_v[entry, 0], tr_v[entry, 1]
                columns = slice(child * LANES, (child + 1) * LANES)
                top = jnp.concatenate([real, -imag], axis=1)
                bottom = jnp.concatenate([imag, real], axis=1)
                for part, rows in enumerate((top, bottom)):
                    high, rest = split_two(rows)
                    at = (side * 2 + part) * rank
                    mat_hi[level, q, at : at + rank, columns] = high.astype(jnp.bfloat16)
                    mat_lo[level, q, at : at + rank, columns] = rest.astype(jnp.bfloat16)

    to_place = [(level, q) for level in range(levels) for q in range(boxes // 2)]
    per_pair = -(-len(to_place) // pairs)

    leaves = []
    for h in range(chunks):
        loads[h].wait()
        if h == chunks - 1:
            level_load.wait()
            tr_load.wait()
        width = bands * LANES
        freq = lax.broadcasted_iota(jnp.int32, (width, LANES), 0) + h * width
        if h == 0:
            for load in band_loads:
                load.wait()
        keep = (freq >= band_v[0]) & (freq < band_v[1])
        for pair in range(pairs):
            if h == 0:
                x_loads[2 * pair].wait()
                x_loads[2 * pair + 1].wait()
            if h == chunks - 1:
                for level, q in to_place[pair * per_pair : (pair + 1) * per_pair]:
                    place_matrices(level, q)
            rows = jnp.dot(tab_v[h], x_v[pair], preferred_element_type=jnp.float32)
            for part in range(2):
                for k in range(2):
                    piece = rows[part * width : (part + 1) * width, k * LANES : (k + 1) * LANES]
                    piece = jnp.where(keep, piece, 0.0).astype(jnp.bfloat16)
                    j = 2 * pair + k
                    for g in range(bands):
                        spec_v[
                            h * bands + g,
                            j * LANES : (j + 1) * LANES,
                            part * LANES : (part + 1) * LANES,
                        ] = piece[g * LANES : (g + 1) * LANES]
        if h == 0:
            q_load.wait()
        for g in range(h * bands, (h + 1) * bands):
            left = jnp.concatenate(
                [q_v[j, :, g * LANES : (g + 1) * LANES] for j in range(traces)], axis=1
            )
            both = jnp.dot(left, spec_v[g], preferred_element_type=jnp.float32)
            real = both[:rank, :LANES] - both[rank:, LANES:]
            imag = both[rank:, :LANES] + both[:rank, LANES:]
            leaves.append(jnp.concatenate([real, imag], axis=0))

    def apply(level, q, packed):
        depth = packed.shape[0]
        main = jnp.dot(mat_hi[level, q, :, :depth], packed, preferred_element_type=jnp.float32)
        rest = jnp.dot(
            mat_lo[level, q, :, :depth], packed[:, :LANES], preferred_element_type=jnp.float32
        )
        return main[:, :LANES] + (main[:, LANES:] + rest)

    def packed_two(value):
        return jnp.concatenate(split_two(value), axis=1).astype(jnp.bfloat16)

    now = [None] * boxes
    for level in range(levels):
        stride = 2**level
        lowers = [b for b in range(boxes) if b // stride % 2 == 0]
        before = now[:]
        for q, lower in enumerate(lowers):
            if level == 0:
                packed = packed_two(leaves[q])
            else:
                packed = jnp.concatenate([before[lower], before[lower + stride]], axis=0)
            both = apply(level, q, packed)
            for side in range(2):
                mine = both[side * LANES : (side + 1) * LANES]
                box = lower + side * stride
                if level < levels - 1:
                    now[box] = packed_two(mine)
                else:
                    for s in range(sub_count):
                        for part in range(2):
                            at = part * rank + s * half
                            send[box * sub_count + s, part * half : (part + 1) * half] = mine[
                                at : at + half
                            ].astype(jnp.bfloat16)

    pl.semaphore_wait(barrier, devices - 1)
    copies = []
    for i, offset in enumerate(offsets):
        tt, pp, uu = place(offset)
        copy = pltpu.make_async_remote_copy(
            src_ref=send.at[(tt * space_count + pp) * sub_count + uu],
            dst_ref=recv.at[i],
            send_sem=send_sem.at[i],
            recv_sem=recv_sem.at[i],
            device_id={"trace": tt, "space": pp, "sub": uu},
            device_id_type=pl.DeviceIdType.MESH,
        )
        copy.start()
        copies.append(copy)
    total = send[me].astype(jnp.float32)
    for i in reversed(range(len(offsets))):
        copies[i].wait_recv()
        total = total + recv[i].astype(jnp.float32)
    out_ref[...] = total.reshape(1, 2, half, LANES)
    for copy in copies:
        copy.wait_send()


def fused_device(seismic, band_low, band_high, leaf_weights, translations, level_table):
    sizes = tuple(lax.axis_size(name) for name in ("trace", "space", "sub"))
    devices = math.prod(sizes)
    boxes = sizes[0] * sizes[1]
    traces, samples, shots = seismic.shape
    freq_total, rank = leaf_weights.shape[1], leaf_weights.shape[3]
    chunks = 2
    levels = level_table.shape[0]
    table = jnp.asarray(table_rows(freq_total, samples, chunks))
    weights = leaf_weights.transpose(0, 2, 3, 1).reshape(traces, 2 * rank, freq_total)
    half = rank // sizes[2]
    hbm_spec = pl.BlockSpec(memory_space=pltpu.HBM)
    vmem_spec = pl.BlockSpec(memory_space=pltpu.VMEM)
    dma = pltpu.SemaphoreType.DMA
    return pl.pallas_call(
        functools.partial(fused_kernel, sizes),
        out_shape=jax.ShapeDtypeStruct((1, 2, rank // sizes[2], shots), jnp.float32),
        in_specs=[hbm_spec] * 7,
        out_specs=vmem_spec,
        scratch_shapes=[
            pltpu.VMEM((2, 1, shots), jnp.int32),
            pltpu.SMEM((levels, 2, boxes), jnp.int32),
            pltpu.VMEM((traces // 2, samples, 2 * shots), jnp.bfloat16),
            pltpu.VMEM(weights.shape, jnp.bfloat16),
            pltpu.VMEM(table.shape, jnp.bfloat16),
            pltpu.VMEM(translations.shape, jnp.float32),
            pltpu.VMEM((sizes[0], traces * LANES, 2 * LANES), jnp.bfloat16),
            pltpu.VMEM((levels, boxes // 2, 4 * rank, 4 * rank), jnp.bfloat16),
            pltpu.VMEM((levels, boxes // 2, 4 * rank, 4 * rank), jnp.bfloat16),
            pltpu.VMEM((devices, 2 * half, shots), jnp.bfloat16),
            pltpu.VMEM((devices - 1, 2 * half, shots), jnp.bfloat16),
            dma((chunks + traces + 2,)),
            dma((3,)),
            dma((devices - 1,)),
            dma((devices - 1,)),
        ],
        compiler_params=pltpu.CompilerParams(
            collective_id=0, has_side_effects=True, vmem_limit_bytes=56 * 2**20
        ),
    )(
        seismic,
        band_low.reshape(1, shots),
        band_high.reshape(1, shots),
        weights,
        table,
        translations,
        level_table.transpose(0, 2, 1),
    )


def per_device(seismic, band_low, band_high, leaf_weights, translations, level_table):
    trace_count, space_count, sub_count = (
        lax.axis_size(name) for name in ("trace", "space", "sub")
    )
    devices = trace_count * space_count * sub_count
    traces, _, shots = seismic.shape
    freq_total, rank = leaf_weights.shape[1], leaf_weights.shape[3]
    fits = (
        shots == LANES
        and freq_total == trace_count * LANES
        and 2 * rank == LANES
        and space_count == 2
        and traces % 2 == 0
        and trace_count % 2 == 0
    )
    chosen = fused_device if fits else general_device
    return chosen(seismic, band_low, band_high, leaf_weights, translations, level_table)


def solution(mesh):
    placed = (
        P(("groups", "trace", "space", "sub"), None, None),
        P("groups"),
        P("groups"),
        P(),
        P(),
        P(),
    )
    return jax.shard_map(
        per_device,
        mesh=mesh,
        in_specs=placed,
        out_specs=P(("groups", "trace", "space"), None, "sub", None),
        check_vma=False,
    )
```

```python
import functools
import math

import jax
import jax.numpy as jnp
import ml_dtypes
import numpy as np
from jax import lax
from jax.experimental import pallas as pl
from jax.experimental.pallas import tpu as pltpu
from jax.sharding import PartitionSpec as P

LANES = 128


def swapped(x, axis, distance):
    return lax.ppermute(x, axis, [(i, i ^ 1 << distance) for i in range(lax.axis_size(axis))])


def spectral_table(freq_total, samples):
    freq_range = jnp.arange(freq_total, dtype=jnp.int32)
    time_range = jnp.arange(samples, dtype=jnp.int32)
    phase = freq_range[:, None] * time_range[None, :] % samples
    angle = phase.astype(jnp.float32) * (2.0 * math.pi / samples)
    factor = 1.0 / math.sqrt(samples)
    return (jnp.concatenate([jnp.cos(angle), -jnp.sin(angle)], axis=0) * factor).astype(
        jnp.bfloat16
    )


def complex_product(left, right):
    highest = lax.Precision.HIGHEST
    real_part = jnp.dot(left[0], right[0], precision=highest) - jnp.dot(
        left[1], right[1], precision=highest
    )
    imag_part = jnp.dot(left[0], right[1], precision=highest) + jnp.dot(
        left[1], right[0], precision=highest
    )
    return jnp.stack([real_part, imag_part])


def swap_space(weights_now, bit_no):
    return swapped(weights_now, "space", bit_no)


def swap_trace(weights_now, bit_no):
    return swapped(weights_now, "trace", bit_no)


def merge_level(
    weights_now, partner, section_no, box_index, translations, level_table, sub_place, half_rank
):
    stride = 2**section_no
    upper_flag = box_index // stride % 2 == 1
    lower_part = jnp.where(upper_flag, partner, weights_now)
    upper_part = jnp.where(upper_flag, weights_now, partner)
    entries = lax.dynamic_index_in_dim(level_table[section_no], box_index, 0, keepdims=False)
    first_mat = lax.dynamic_index_in_dim(translations, entries[0], 0, keepdims=False)
    second_mat = lax.dynamic_index_in_dim(translations, entries[1], 0, keepdims=False)
    full_lower, full_upper = (
        lax.all_gather(lower_part, "sub", axis=1, tiled=True),
        lax.all_gather(upper_part, "sub", axis=1, tiled=True),
    )
    first_rows = lax.dynamic_slice_in_dim(first_mat, sub_place * half_rank, half_rank, 1)
    second_rows = lax.dynamic_slice_in_dim(second_mat, sub_place * half_rank, half_rank, 1)
    return complex_product(first_rows, full_lower) + complex_product(second_rows, full_upper)


def join_complex(parts):
    return jnp.stack([parts[:, 0, 0] - parts[:, 1, 1], parts[:, 0, 1] + parts[:, 1, 0]], axis=1)


def general_device(seismic, band_low, band_high, leaf_weights, translations, level_table):
    highest = lax.Precision.HIGHEST
    trace_count = lax.axis_size("trace")
    space_count = lax.axis_size("space")
    sub_count = lax.axis_size("sub")
    trace_place = lax.axis_index("trace")
    space_place = lax.axis_index("space")
    sub_place = lax.axis_index("sub")
    traces_here = seismic.shape[0]
    samples = seismic.shape[1]
    shots_count = seismic.shape[2]
    freq_total = leaf_weights.shape[1]
    rank_total = leaf_weights.shape[3]
    freq_block = freq_total // trace_count
    half_rank = rank_total // sub_count
    dft_rows = spectral_table(freq_total, samples)
    spectra = jnp.einsum(
        "kt,xts->xks", dft_rows, seismic, preferred_element_type=jnp.float32
    ).astype(jnp.bfloat16)
    spectra = spectra.reshape(traces_here, 2, freq_total, shots_count)
    freq_index = jnp.arange(freq_total, dtype=jnp.int32)
    band_mask = (
        (freq_index[:, None] >= band_low[None, :]) & (freq_index[:, None] < band_high[None, :])
    ).astype(jnp.bfloat16)
    masked = spectra * band_mask
    piece = masked.astype(jnp.float32)
    piece = piece.reshape(traces_here, 2, 1 * lax.axis_size("trace"), freq_block, shots_count)
    leaf_piece = leaf_weights.astype(jnp.float32)
    leaf_piece = leaf_piece.reshape(
        traces_here, 1 * lax.axis_size("trace"), freq_block, 2, rank_total
    )
    parts = jnp.einsum("iagfs,igfbr->gabrs", piece, leaf_piece, precision=highest)
    leaf_terms = lax.psum_scatter(join_complex(parts), "trace", scatter_dimension=0, tiled=True)[0]
    weights_now = lax.psum_scatter(leaf_terms, "sub", scatter_dimension=1, tiled=True)
    box_index = trace_place * space_count + space_place
    section_no = 0
    for bit_no in range(space_count.bit_length() - 1):
        partner = swap_space(weights_now, bit_no)
        weights_now = merge_level(
            weights_now,
            partner,
            section_no,
            box_index,
            translations,
            level_table,
            sub_place,
            half_rank,
        )
        section_no = section_no + 1
    for bit_no in range(trace_count.bit_length() - 1):
        partner = swap_trace(weights_now, bit_no)
        weights_now = merge_level(
            weights_now,
            partner,
            section_no,
            box_index,
            translations,
            level_table,
            sub_place,
            half_rank,
        )
        section_no = section_no + 1
    return weights_now[None]


def table_rows(freq_total, samples, chunks):
    phase = np.arange(freq_total)[:, None] * np.arange(samples)[None, :] % samples
    angle = phase.astype(np.float32) * np.float32(2.0 * math.pi / samples)
    factor = np.float32(1.0 / math.sqrt(samples))
    parts = np.stack([np.cos(angle), -np.sin(angle)]) * factor
    rows = parts.reshape(2, chunks, freq_total // chunks, samples).transpose(1, 0, 2, 3)
    return rows.reshape(chunks, 2 * freq_total // chunks, samples).astype(ml_dtypes.bfloat16)


def split_two(x):
    high = x.astype(jnp.bfloat16).astype(jnp.float32)
    return high, x - high


def fused_kernel(
    sizes,
    x_hbm,
    low_hbm,
    high_hbm,
    q_hbm,
    tab_hbm,
    tr_hbm,
    level_hbm,
    out_ref,
    band_v,
    level_ref,
    x_v,
    q_v,
    tab_v,
    tr_v,
    spec_v,
    mat_hi,
    mat_lo,
    own,
    give,
    near,
    send,
    recv,
    load_sem,
    small_sem,
    near_send_sem,
    near_recv_sem,
    send_sem,
    recv_sem,
):
    trace_count, space_count, sub_count = sizes
    t, p, u = lax.axis_index("trace"), lax.axis_index("space"), lax.axis_index("sub")
    chunks = tab_v.shape[0]
    traces = q_v.shape[0]
    pairs = traces // 2
    bands = trace_count // chunks
    boxes = trace_count * space_count
    levels = mat_hi.shape[0]
    rank = tr_v.shape[2]
    half = rank // sub_count

    band_loads = [
        pltpu.make_async_copy(low_hbm, band_v.at[0], small_sem.at[0]),
        pltpu.make_async_copy(high_hbm, band_v.at[1], small_sem.at[1]),
    ]
    level_load = pltpu.make_async_copy(level_hbm, level_ref, small_sem.at[2])
    loads = []
    for h in range(chunks):
        loads.append(pltpu.make_async_copy(tab_hbm.at[h], tab_v.at[h], load_sem.at[len(loads)]))
    x_loads = []
    for j in range(traces):
        x_loads.append(
            pltpu.make_async_copy(
                x_hbm.at[j],
                x_v.at[j // 2, :, pl.ds(j % 2 * LANES, LANES)],
                load_sem.at[chunks + j],
            )
        )
    q_load = pltpu.make_async_copy(q_hbm, q_v, load_sem.at[chunks + traces])
    tr_load = pltpu.make_async_copy(tr_hbm, tr_v, load_sem.at[chunks + traces + 1])
    loads[0].start()
    for load in x_loads:
        load.start()
    for load in band_loads:
        load.start()
    q_load.start()
    for load in loads[1:]:
        load.start()
    level_load.start()
    tr_load.start()

    offsets = [
        (dt, dp) for dt in range(trace_count) for dp in range(space_count) if dt or dp
    ]
    offsets.sort(key=lambda o: -min(o[0], trace_count - o[0]) * 2 - o[1])

    def place(offset):
        return lax.rem(t + offset[0], trace_count), lax.rem(p + offset[1], space_count)

    sibling = {"sub": 1 - u}
    barrier = pltpu.get_barrier_semaphore()
    pl.semaphore_signal(
        barrier, inc=1, device_id=sibling, device_id_type=pl.DeviceIdType.MESH
    )
    for offset in offsets:
        tt, pp = place(offset)
        pl.semaphore_signal(
            barrier,
            inc=1,
            device_id={"trace": tt, "space": pp},
            device_id_type=pl.DeviceIdType.MESH,
        )

    def place_matrices(level, q):
        stride = 2**level
        lower = [b for b in range(boxes) if b // stride % 2 == 0][q]
        for side in range(2):
            for child in range(2 if level else 1):
                entry = level_ref[level, child if level else p, lower + side * stride]
                real, imag = tr_v[entry, 0], tr_v[entry, 1]
                columns = slice(child * LANES, (child + 1) * LANES)
                top = jnp.concatenate([real, -imag], axis=1)
                bottom = jnp.concatenate([imag, real], axis=1)
                for part, rows in enumerate((top, bottom)):
                    high, rest = split_two(rows)
                    at = (side * 2 + part) * rank
                    mat_hi[level, q, at : at + rank, columns] = high.astype(jnp.bfloat16)
                    mat_lo[level, q, at : at + rank, columns] = rest.astype(jnp.bfloat16)

    to_place = [(level, q) for level in range(levels) for q in range(boxes // 2)]
    per_pair = -(-len(to_place) // pairs)

    leaves = []
    for h in range(chunks):
        loads[h].wait()
        if h == chunks - 1:
            level_load.wait()
            tr_load.wait()
        width = bands * LANES
        freq = lax.broadcasted_iota(jnp.int32, (width, LANES), 0) + h * width
        if h == 0:
            for load in band_loads:
                load.wait()
        keep = (freq >= band_v[0]) & (freq < band_v[1])
        for pair in range(pairs):
            if h == 0:
                x_loads[2 * pair].wait()
                x_loads[2 * pair + 1].wait()
            if h == chunks - 1:
                for level, q in to_place[pair * per_pair : (pair + 1) * per_pair]:
                    place_matrices(level, q)
            rows = jnp.dot(tab_v[h], x_v[pair], preferred_element_type=jnp.float32)
            for part in range(2):
                for k in range(2):
                    piece = rows[part * width : (part + 1) * width, k * LANES : (k + 1) * LANES]
                    piece = jnp.where(keep, piece, 0.0).astype(jnp.bfloat16)
                    j = 2 * pair + k
                    for g in range(bands):
                        spec_v[
                            h * bands + g,
                            j * LANES : (j + 1) * LANES,
                            part * LANES : (part + 1) * LANES,
                        ] = piece[g * LANES : (g + 1) * LANES]
        if h == 0:
            q_load.wait()
        for g in range(h * bands, (h + 1) * bands):
            left = jnp.concatenate(
                [q_v[j, :, g * LANES : (g + 1) * LANES] for j in range(traces)], axis=1
            )
            both = jnp.dot(left, spec_v[g], preferred_element_type=jnp.float32)
            real = both[:rank, :LANES] - both[rank:, LANES:]
            imag = both[rank:, :LANES] + both[:rank, LANES:]
            leaves.append(jnp.concatenate([real, imag], axis=0))

    def apply(level, q, packed):
        depth = packed.shape[0]
        main = jnp.dot(mat_hi[level, q, :, :depth], packed, preferred_element_type=jnp.float32)
        rest = jnp.dot(
            mat_lo[level, q, :, :depth], packed[:, :LANES], preferred_element_type=jnp.float32
        )
        return main[:, :LANES] + (main[:, LANES:] + rest)

    def packed_two(value):
        return jnp.concatenate(split_two(value), axis=1).astype(jnp.bfloat16)

    def near_copy(box):
        return pltpu.make_async_remote_copy(
            src_ref=give.at[box],
            dst_ref=near.at[box],
            send_sem=near_send_sem.at[box],
            recv_sem=near_recv_sem.at[box],
            device_id=sibling,
            device_id_type=pl.DeviceIdType.MESH,
        )

    now = [None] * boxes
    for level in range(levels):
        if level == levels - 1:
            pl.semaphore_wait(barrier, len(offsets) + 1)
        stride = 2**level
        lowers = [b for b in range(boxes) if b // stride % 2 == 0]
        before = now[:]
        for q, lower in enumerate(lowers):
            if level == 0:
                packed = packed_two(leaves[q])
            else:
                packed = jnp.concatenate([before[lower], before[lower + stride]], axis=0)
            both = apply(level, q, packed)
            for side in range(2):
                mine = both[side * LANES : (side + 1) * LANES]
                box = lower + side * stride
                if level < levels - 1:
                    now[box] = packed_two(mine)
                else:
                    for part in range(2):
                        first, second = (
                            mine[part * rank + s * half : part * rank + (s + 1) * half]
                            for s in range(2)
                        )
                        rows = slice(part * half, (part + 1) * half)
                        own[box, rows] = jnp.where(u == 0, first, second)
                        give[box, rows] = jnp.where(u == 0, second, first).astype(jnp.bfloat16)
                    near_copy(box).start()

    def summed(box):
        near_copy(box).wait_recv()
        return own[box] + near[box].astype(jnp.float32)

    copies = []
    for i, offset in enumerate(offsets):
        tt, pp = place(offset)
        send[i] = summed(tt * space_count + pp).astype(jnp.bfloat16)
        copy = pltpu.make_async_remote_copy(
            src_ref=send.at[i],
            dst_ref=recv.at[i],
            send_sem=send_sem.at[i],
            recv_sem=recv_sem.at[i],
            device_id={"trace": tt, "space": pp},
            device_id_type=pl.DeviceIdType.MESH,
        )
        copy.start()
        copies.append(copy)
    total = summed(t * space_count + p)
    for i in reversed(range(len(offsets))):
        copies[i].wait_recv()
        total = total + recv[i].astype(jnp.float32)
    out_ref[...] = total.reshape(1, 2, half, LANES)
    for box in range(boxes):
        near_copy(box).wait_send()
    for copy in copies:
        copy.wait_send()


def fused_device(seismic, band_low, band_high, leaf_weights, translations, level_table):
    sizes = tuple(lax.axis_size(name) for name in ("trace", "space", "sub"))
    boxes = sizes[0] * sizes[1]
    traces, samples, shots = seismic.shape
    freq_total, rank = leaf_weights.shape[1], leaf_weights.shape[3]
    chunks = 2
    levels = level_table.shape[0]
    table = jnp.asarray(table_rows(freq_total, samples, chunks))
    weights = leaf_weights.transpose(0, 2, 3, 1).reshape(traces, 2 * rank, freq_total)
    half = rank // sizes[2]
    hbm_spec = pl.BlockSpec(memory_space=pltpu.HBM)
    vmem_spec = pl.BlockSpec(memory_space=pltpu.VMEM)
    dma = pltpu.SemaphoreType.DMA
    return pl.pallas_call(
        functools.partial(fused_kernel, sizes),
        out_shape=jax.ShapeDtypeStruct((1, 2, rank // sizes[2], shots), jnp.float32),
        in_specs=[hbm_spec] * 7,
        out_specs=vmem_spec,
        scratch_shapes=[
            pltpu.VMEM((2, 1, shots), jnp.int32),
            pltpu.SMEM((levels, 2, boxes), jnp.int32),
            pltpu.VMEM((traces // 2, samples, 2 * shots), jnp.bfloat16),
            pltpu.VMEM(weights.shape, jnp.bfloat16),
            pltpu.VMEM(table.shape, jnp.bfloat16),
            pltpu.VMEM(translations.shape, jnp.float32),
            pltpu.VMEM((sizes[0], traces * LANES, 2 * LANES), jnp.bfloat16),
            pltpu.VMEM((levels, boxes // 2, 4 * rank, 4 * rank), jnp.bfloat16),
            pltpu.VMEM((levels, boxes // 2, 4 * rank, 4 * rank), jnp.bfloat16),
            pltpu.VMEM((boxes, 2 * half, shots), jnp.float32),
            pltpu.VMEM((boxes, 2 * half, shots), jnp.bfloat16),
            pltpu.VMEM((boxes, 2 * half, shots), jnp.bfloat16),
            pltpu.VMEM((boxes - 1, 2 * half, shots), jnp.bfloat16),
            pltpu.VMEM((boxes - 1, 2 * half, shots), jnp.bfloat16),
            dma((chunks + traces + 2,)),
            dma((3,)),
            dma((boxes,)),
            dma((boxes,)),
            dma((boxes - 1,)),
            dma((boxes - 1,)),
        ],
        compiler_params=pltpu.CompilerParams(
            collective_id=0, has_side_effects=True, vmem_limit_bytes=56 * 2**20
        ),
    )(
        seismic,
        band_low.reshape(1, shots),
        band_high.reshape(1, shots),
        weights,
        table,
        translations,
        level_table.transpose(0, 2, 1),
    )


def per_device(seismic, band_low, band_high, leaf_weights, translations, level_table):
    trace_count, space_count, sub_count = (
        lax.axis_size(name) for name in ("trace", "space", "sub")
    )
    traces, _, shots = seismic.shape
    freq_total, rank = leaf_weights.shape[1], leaf_weights.shape[3]
    fits = (
        shots == LANES
        and freq_total == trace_count * LANES
        and 2 * rank == LANES
        and space_count == 2
        and sub_count == 2
        and traces % 2 == 0
        and trace_count % 2 == 0
    )
    chosen = fused_device if fits else general_device
    return chosen(seismic, band_low, band_high, leaf_weights, translations, level_table)


def solution(mesh):
    placed = (
        P(("groups", "trace", "space", "sub"), None, None),
        P("groups"),
        P("groups"),
        P(),
        P(),
        P(),
    )
    return jax.shard_map(
        per_device,
        mesh=mesh,
        in_specs=placed,
        out_specs=P(("groups", "trace", "space"), None, "sub", None),
        check_vma=False,
    )
```

```python
import functools
import math

import jax
import jax.numpy as jnp
import ml_dtypes
import numpy as np
from jax import lax
from jax.experimental import pallas as pl
from jax.experimental.pallas import tpu as pltpu
from jax.sharding import PartitionSpec as P

LANES = 128


def swapped(x, axis, distance):
    return lax.ppermute(x, axis, [(i, i ^ 1 << distance) for i in range(lax.axis_size(axis))])


def spectral_table(freq_total, samples):
    freq_range = jnp.arange(freq_total, dtype=jnp.int32)
    time_range = jnp.arange(samples, dtype=jnp.int32)
    phase = freq_range[:, None] * time_range[None, :] % samples
    angle = phase.astype(jnp.float32) * (2.0 * math.pi / samples)
    factor = 1.0 / math.sqrt(samples)
    return (jnp.concatenate([jnp.cos(angle), -jnp.sin(angle)], axis=0) * factor).astype(
        jnp.bfloat16
    )


def complex_product(left, right):
    highest = lax.Precision.HIGHEST
    real_part = jnp.dot(left[0], right[0], precision=highest) - jnp.dot(
        left[1], right[1], precision=highest
    )
    imag_part = jnp.dot(left[0], right[1], precision=highest) + jnp.dot(
        left[1], right[0], precision=highest
    )
    return jnp.stack([real_part, imag_part])


def swap_space(weights_now, bit_no):
    return swapped(weights_now, "space", bit_no)


def swap_trace(weights_now, bit_no):
    return swapped(weights_now, "trace", bit_no)


def merge_level(
    weights_now, partner, section_no, box_index, translations, level_table, sub_place, half_rank
):
    stride = 2**section_no
    upper_flag = box_index // stride % 2 == 1
    lower_part = jnp.where(upper_flag, partner, weights_now)
    upper_part = jnp.where(upper_flag, weights_now, partner)
    entries = lax.dynamic_index_in_dim(level_table[section_no], box_index, 0, keepdims=False)
    first_mat = lax.dynamic_index_in_dim(translations, entries[0], 0, keepdims=False)
    second_mat = lax.dynamic_index_in_dim(translations, entries[1], 0, keepdims=False)
    full_lower, full_upper = (
        lax.all_gather(lower_part, "sub", axis=1, tiled=True),
        lax.all_gather(upper_part, "sub", axis=1, tiled=True),
    )
    first_rows = lax.dynamic_slice_in_dim(first_mat, sub_place * half_rank, half_rank, 1)
    second_rows = lax.dynamic_slice_in_dim(second_mat, sub_place * half_rank, half_rank, 1)
    return complex_product(first_rows, full_lower) + complex_product(second_rows, full_upper)


def join_complex(parts):
    return jnp.stack([parts[:, 0, 0] - parts[:, 1, 1], parts[:, 0, 1] + parts[:, 1, 0]], axis=1)


def general_device(seismic, band_low, band_high, leaf_weights, translations, level_table):
    highest = lax.Precision.HIGHEST
    trace_count = lax.axis_size("trace")
    space_count = lax.axis_size("space")
    sub_count = lax.axis_size("sub")
    trace_place = lax.axis_index("trace")
    space_place = lax.axis_index("space")
    sub_place = lax.axis_index("sub")
    traces_here = seismic.shape[0]
    samples = seismic.shape[1]
    shots_count = seismic.shape[2]
    freq_total = leaf_weights.shape[1]
    rank_total = leaf_weights.shape[3]
    freq_block = freq_total // trace_count
    half_rank = rank_total // sub_count
    dft_rows = spectral_table(freq_total, samples)
    spectra = jnp.einsum(
        "kt,xts->xks", dft_rows, seismic, preferred_element_type=jnp.float32
    ).astype(jnp.bfloat16)
    spectra = spectra.reshape(traces_here, 2, freq_total, shots_count)
    freq_index = jnp.arange(freq_total, dtype=jnp.int32)
    band_mask = (
        (freq_index[:, None] >= band_low[None, :]) & (freq_index[:, None] < band_high[None, :])
    ).astype(jnp.bfloat16)
    masked = spectra * band_mask
    piece = masked.astype(jnp.float32)
    piece = piece.reshape(traces_here, 2, 1 * lax.axis_size("trace"), freq_block, shots_count)
    leaf_piece = leaf_weights.astype(jnp.float32)
    leaf_piece = leaf_piece.reshape(
        traces_here, 1 * lax.axis_size("trace"), freq_block, 2, rank_total
    )
    parts = jnp.einsum("iagfs,igfbr->gabrs", piece, leaf_piece, precision=highest)
    leaf_terms = lax.psum_scatter(join_complex(parts), "trace", scatter_dimension=0, tiled=True)[0]
    weights_now = lax.psum_scatter(leaf_terms, "sub", scatter_dimension=1, tiled=True)
    box_index = trace_place * space_count + space_place
    section_no = 0
    for bit_no in range(space_count.bit_length() - 1):
        partner = swap_space(weights_now, bit_no)
        weights_now = merge_level(
            weights_now,
            partner,
            section_no,
            box_index,
            translations,
            level_table,
            sub_place,
            half_rank,
        )
        section_no = section_no + 1
    for bit_no in range(trace_count.bit_length() - 1):
        partner = swap_trace(weights_now, bit_no)
        weights_now = merge_level(
            weights_now,
            partner,
            section_no,
            box_index,
            translations,
            level_table,
            sub_place,
            half_rank,
        )
        section_no = section_no + 1
    return weights_now[None]


def table_rows(freq_total, samples, chunks):
    phase = np.arange(freq_total)[:, None] * np.arange(samples)[None, :] % samples
    angle = phase.astype(np.float32) * np.float32(2.0 * math.pi / samples)
    factor = np.float32(1.0 / math.sqrt(samples))
    parts = np.stack([np.cos(angle), -np.sin(angle)]) * factor
    rows = parts.reshape(2, chunks, freq_total // chunks, samples).transpose(1, 0, 2, 3)
    return rows.reshape(chunks, 2 * freq_total // chunks, samples).astype(ml_dtypes.bfloat16)


def split_two(x):
    high = x.astype(jnp.bfloat16).astype(jnp.float32)
    return high, x - high


def fused_kernel(
    sizes,
    x_hbm,
    low_hbm,
    high_hbm,
    q_hbm,
    tab_hbm,
    tr_hbm,
    level_hbm,
    out_ref,
    band_v,
    level_ref,
    x_v,
    q_v,
    tab_v,
    tr_v,
    spec_v,
    mat_hi,
    mat_lo,
    own,
    give,
    near,
    send,
    recv,
    load_sem,
    small_sem,
    near_send_sem,
    near_recv_sem,
    send_sem,
    recv_sem,
):
    trace_count, space_count, sub_count = sizes
    t, p, u = lax.axis_index("trace"), lax.axis_index("space"), lax.axis_index("sub")
    chunks = tab_v.shape[0]
    traces = q_v.shape[0]
    pairs = traces // 2
    bands = trace_count // chunks
    boxes = trace_count * space_count
    levels = mat_hi.shape[0]
    rank = tr_v.shape[2]
    half = rank // sub_count

    band_loads = [
        pltpu.make_async_copy(low_hbm, band_v.at[0], small_sem.at[0]),
        pltpu.make_async_copy(high_hbm, band_v.at[1], small_sem.at[1]),
    ]
    level_load = pltpu.make_async_copy(level_hbm, level_ref, small_sem.at[2])
    slabs = 4
    slab = tab_v.shape[1] // slabs
    tab_loads = [
        pltpu.make_async_copy(
            tab_hbm.at[0, pl.ds(n * slab, slab)], tab_v.at[0, pl.ds(n * slab, slab)], load_sem.at[n]
        )
        for n in range(slabs)
    ]
    x_loads = []
    for j in range(traces):
        x_loads.append(
            pltpu.make_async_copy(
                x_hbm.at[j],
                x_v.at[j // 2, :, pl.ds(j % 2 * LANES, LANES)],
                load_sem.at[slabs + j],
            )
        )
    q_load = pltpu.make_async_copy(q_hbm, q_v, load_sem.at[slabs + traces])
    tr_load = pltpu.make_async_copy(tr_hbm, tr_v, load_sem.at[slabs + traces + 1])
    for load in band_loads + x_loads[:2] + tab_loads + x_loads[2:] + [level_load]:
        load.start()

    offsets = [
        (dt, dp) for dt in range(trace_count) for dp in range(space_count) if dt or dp
    ]
    offsets.sort(key=lambda o: -min(o[0], trace_count - o[0]) * 2 - o[1])

    def place(offset):
        return lax.rem(t + offset[0], trace_count), lax.rem(p + offset[1], space_count)

    sibling = {"sub": 1 - u}
    barrier = pltpu.get_barrier_semaphore()
    pl.semaphore_signal(
        barrier, inc=1, device_id=sibling, device_id_type=pl.DeviceIdType.MESH
    )
    for offset in offsets:
        tt, pp = place(offset)
        pl.semaphore_signal(
            barrier,
            inc=1,
            device_id={"trace": tt, "space": pp},
            device_id_type=pl.DeviceIdType.MESH,
        )

    def place_matrices(level, q):
        stride = 2**level
        lower = [b for b in range(boxes) if b // stride % 2 == 0][q]
        for side in range(2):
            for child in range(2 if level else 1):
                entry = level_ref[level, child if level else p, lower + side * stride]
                real, imag = tr_v[entry, 0], tr_v[entry, 1]
                columns = slice(child * LANES, (child + 1) * LANES)
                top = jnp.concatenate([real, -imag], axis=1)
                bottom = jnp.concatenate([imag, real], axis=1)
                for part, rows in enumerate((top, bottom)):
                    high, rest = split_two(rows)
                    at = (side * 2 + part) * rank
                    mat_hi[level, q, at : at + rank, columns] = high.astype(jnp.bfloat16)
                    mat_lo[level, q, at : at + rank, columns] = rest.astype(jnp.bfloat16)

    to_place = [(level, q) for level in range(levels) for q in range(boxes // 2)]
    per_pair = -(-len(to_place) // (pairs - 1))

    leaves = []
    for h in range(chunks):
        for load in tab_loads:
            load.wait()
        width = bands * LANES
        freq = lax.broadcasted_iota(jnp.int32, (width, LANES), 0) + h * width
        if h == 0:
            for load in band_loads:
                load.wait()
        keep = (freq >= band_v[0]) & (freq < band_v[1])
        for pair in range(pairs):
            x_loads[2 * pair].wait()
            x_loads[2 * pair + 1].wait()
            if pair == 0:
                tr_load.start()
                q_load.start()
            if pair == 1:
                level_load.wait()
                tr_load.wait()
            if pair >= 1:
                for level, q in to_place[(pair - 1) * per_pair : pair * per_pair]:
                    place_matrices(level, q)
            rows = jnp.dot(tab_v[h], x_v[pair], preferred_element_type=jnp.float32)
            for part in range(2):
                for k in range(2):
                    piece = rows[part * width : (part + 1) * width, k * LANES : (k + 1) * LANES]
                    piece = jnp.where(keep, piece, 0.0).astype(jnp.bfloat16)
                    j = 2 * pair + k
                    for g in range(bands):
                        spec_v[
                            h * bands + g,
                            j * LANES : (j + 1) * LANES,
                            part * LANES : (part + 1) * LANES,
                        ] = piece[g * LANES : (g + 1) * LANES]
        q_load.wait()
        for g in range(h * bands, (h + 1) * bands):
            left = jnp.concatenate(
                [q_v[j, :, g * LANES : (g + 1) * LANES] for j in range(traces)], axis=1
            )
            both = jnp.dot(left, spec_v[g], preferred_element_type=jnp.float32)
            real = both[:rank, :LANES] - both[rank:, LANES:]
            imag = both[rank:, :LANES] + both[:rank, LANES:]
            leaves.append(jnp.concatenate([real, imag], axis=0))

    def apply(level, q, packed):
        depth = packed.shape[0]
        main = jnp.dot(mat_hi[level, q, :, :depth], packed, preferred_element_type=jnp.float32)
        rest = jnp.dot(
            mat_lo[level, q, :, :depth], packed[:, :LANES], preferred_element_type=jnp.float32
        )
        return main[:, :LANES] + (main[:, LANES:] + rest)

    def packed_two(value):
        return jnp.concatenate(split_two(value), axis=1).astype(jnp.bfloat16)

    def near_copy(box):
        return pltpu.make_async_remote_copy(
            src_ref=give.at[box],
            dst_ref=near.at[box],
            send_sem=near_send_sem.at[box],
            recv_sem=near_recv_sem.at[box],
            device_id=sibling,
            device_id_type=pl.DeviceIdType.MESH,
        )

    now = [None] * boxes
    for level in range(levels):
        if level == levels - 1:
            pl.semaphore_wait(barrier, len(offsets) + 1)
        stride = 2**level
        lowers = [b for b in range(boxes) if b // stride % 2 == 0]
        before = now[:]
        for q, lower in enumerate(lowers):
            if level == 0:
                packed = packed_two(leaves[q])
            else:
                packed = jnp.concatenate([before[lower], before[lower + stride]], axis=0)
            both = apply(level, q, packed)
            for side in range(2):
                mine = both[side * LANES : (side + 1) * LANES]
                box = lower + side * stride
                if level < levels - 1:
                    now[box] = packed_two(mine)
                else:
                    for part in range(2):
                        first, second = (
                            mine[part * rank + s * half : part * rank + (s + 1) * half]
                            for s in range(2)
                        )
                        rows = slice(part * half, (part + 1) * half)
                        own[box, rows] = jnp.where(u == 0, first, second)
                        give[box, rows] = jnp.where(u == 0, second, first).astype(jnp.bfloat16)
                    near_copy(box).start()

    def summed(box):
        near_copy(box).wait_recv()
        return own[box] + near[box].astype(jnp.float32)

    copies = []
    for i, offset in enumerate(offsets):
        tt, pp = place(offset)
        send[i] = summed(tt * space_count + pp).astype(jnp.bfloat16)
        copy = pltpu.make_async_remote_copy(
            src_ref=send.at[i],
            dst_ref=recv.at[i],
            send_sem=send_sem.at[i],
            recv_sem=recv_sem.at[i],
            device_id={"trace": tt, "space": pp},
            device_id_type=pl.DeviceIdType.MESH,
        )
        copy.start()
        copies.append(copy)
    total = summed(t * space_count + p)
    for i in reversed(range(len(offsets))):
        copies[i].wait_recv()
        total = total + recv[i].astype(jnp.float32)
    out_ref[...] = total.reshape(1, 2, half, LANES)
    for box in range(boxes):
        near_copy(box).wait_send()
    for copy in copies:
        copy.wait_send()


def fused_device(seismic, band_low, band_high, leaf_weights, translations, level_table):
    sizes = tuple(lax.axis_size(name) for name in ("trace", "space", "sub"))
    boxes = sizes[0] * sizes[1]
    traces, samples, shots = seismic.shape
    freq_total, rank = leaf_weights.shape[1], leaf_weights.shape[3]
    chunks = 1
    levels = level_table.shape[0]
    table = jnp.asarray(table_rows(freq_total, samples, chunks))
    weights = leaf_weights.transpose(0, 2, 3, 1).reshape(traces, 2 * rank, freq_total)
    half = rank // sizes[2]
    hbm_spec = pl.BlockSpec(memory_space=pltpu.HBM)
    vmem_spec = pl.BlockSpec(memory_space=pltpu.VMEM)
    dma = pltpu.SemaphoreType.DMA
    return pl.pallas_call(
        functools.partial(fused_kernel, sizes),
        out_shape=jax.ShapeDtypeStruct((1, 2, rank // sizes[2], shots), jnp.float32),
        in_specs=[hbm_spec] * 7,
        out_specs=vmem_spec,
        scratch_shapes=[
            pltpu.VMEM((2, 1, shots), jnp.int32),
            pltpu.SMEM((levels, 2, boxes), jnp.int32),
            pltpu.VMEM((traces // 2, samples, 2 * shots), jnp.bfloat16),
            pltpu.VMEM(weights.shape, jnp.bfloat16),
            pltpu.VMEM(table.shape, jnp.bfloat16),
            pltpu.VMEM(translations.shape, jnp.float32),
            pltpu.VMEM((sizes[0], traces * LANES, 2 * LANES), jnp.bfloat16),
            pltpu.VMEM((levels, boxes // 2, 4 * rank, 4 * rank), jnp.bfloat16),
            pltpu.VMEM((levels, boxes // 2, 4 * rank, 4 * rank), jnp.bfloat16),
            pltpu.VMEM((boxes, 2 * half, shots), jnp.float32),
            pltpu.VMEM((boxes, 2 * half, shots), jnp.bfloat16),
            pltpu.VMEM((boxes, 2 * half, shots), jnp.bfloat16),
            pltpu.VMEM((boxes - 1, 2 * half, shots), jnp.bfloat16),
            pltpu.VMEM((boxes - 1, 2 * half, shots), jnp.bfloat16),
            dma((traces + 6,)),
            dma((3,)),
            dma((boxes,)),
            dma((boxes,)),
            dma((boxes - 1,)),
            dma((boxes - 1,)),
        ],
        compiler_params=pltpu.CompilerParams(
            collective_id=0, has_side_effects=True, vmem_limit_bytes=56 * 2**20
        ),
    )(
        seismic,
        band_low.reshape(1, shots),
        band_high.reshape(1, shots),
        weights,
        table,
        translations,
        level_table.transpose(0, 2, 1),
    )


def per_device(seismic, band_low, band_high, leaf_weights, translations, level_table):
    trace_count, space_count, sub_count = (
        lax.axis_size(name) for name in ("trace", "space", "sub")
    )
    traces, _, shots = seismic.shape
    freq_total, rank = leaf_weights.shape[1], leaf_weights.shape[3]
    fits = (
        shots == LANES
        and freq_total == trace_count * LANES
        and 2 * rank == LANES
        and space_count == 2
        and sub_count == 2
        and traces % 2 == 0
        and traces > 2
        and trace_count % 2 == 0
    )
    chosen = fused_device if fits else general_device
    return chosen(seismic, band_low, band_high, leaf_weights, translations, level_table)


def solution(mesh):
    placed = (
        P(("groups", "trace", "space", "sub"), None, None),
        P("groups"),
        P("groups"),
        P(),
        P(),
        P(),
    )
    return jax.shard_map(
        per_device,
        mesh=mesh,
        in_specs=placed,
        out_specs=P(("groups", "trace", "space"), None, "sub", None),
        check_vma=False,
    )
```

```python
import functools
import math

import jax
import jax.numpy as jnp
import ml_dtypes
import numpy as np
from jax import lax
from jax.experimental import pallas as pl
from jax.experimental.pallas import tpu as pltpu
from jax.sharding import PartitionSpec as P

LANES = 128


def swapped(x, axis, distance):
    return lax.ppermute(x, axis, [(i, i ^ 1 << distance) for i in range(lax.axis_size(axis))])


def spectral_table(freq_total, samples):
    freq_range = jnp.arange(freq_total, dtype=jnp.int32)
    time_range = jnp.arange(samples, dtype=jnp.int32)
    phase = freq_range[:, None] * time_range[None, :] % samples
    angle = phase.astype(jnp.float32) * (2.0 * math.pi / samples)
    factor = 1.0 / math.sqrt(samples)
    return (jnp.concatenate([jnp.cos(angle), -jnp.sin(angle)], axis=0) * factor).astype(
        jnp.bfloat16
    )


def complex_product(left, right):
    highest = lax.Precision.HIGHEST
    real_part = jnp.dot(left[0], right[0], precision=highest) - jnp.dot(
        left[1], right[1], precision=highest
    )
    imag_part = jnp.dot(left[0], right[1], precision=highest) + jnp.dot(
        left[1], right[0], precision=highest
    )
    return jnp.stack([real_part, imag_part])


def swap_space(weights_now, bit_no):
    return swapped(weights_now, "space", bit_no)


def swap_trace(weights_now, bit_no):
    return swapped(weights_now, "trace", bit_no)


def merge_level(
    weights_now, partner, section_no, box_index, translations, level_table, sub_place, half_rank
):
    stride = 2**section_no
    upper_flag = box_index // stride % 2 == 1
    lower_part = jnp.where(upper_flag, partner, weights_now)
    upper_part = jnp.where(upper_flag, weights_now, partner)
    entries = lax.dynamic_index_in_dim(level_table[section_no], box_index, 0, keepdims=False)
    first_mat = lax.dynamic_index_in_dim(translations, entries[0], 0, keepdims=False)
    second_mat = lax.dynamic_index_in_dim(translations, entries[1], 0, keepdims=False)
    full_lower, full_upper = (
        lax.all_gather(lower_part, "sub", axis=1, tiled=True),
        lax.all_gather(upper_part, "sub", axis=1, tiled=True),
    )
    first_rows = lax.dynamic_slice_in_dim(first_mat, sub_place * half_rank, half_rank, 1)
    second_rows = lax.dynamic_slice_in_dim(second_mat, sub_place * half_rank, half_rank, 1)
    return complex_product(first_rows, full_lower) + complex_product(second_rows, full_upper)


def join_complex(parts):
    return jnp.stack([parts[:, 0, 0] - parts[:, 1, 1], parts[:, 0, 1] + parts[:, 1, 0]], axis=1)


def general_device(seismic, band_low, band_high, leaf_weights, translations, level_table):
    highest = lax.Precision.HIGHEST
    trace_count = lax.axis_size("trace")
    space_count = lax.axis_size("space")
    sub_count = lax.axis_size("sub")
    trace_place = lax.axis_index("trace")
    space_place = lax.axis_index("space")
    sub_place = lax.axis_index("sub")
    traces_here = seismic.shape[0]
    samples = seismic.shape[1]
    shots_count = seismic.shape[2]
    freq_total = leaf_weights.shape[1]
    rank_total = leaf_weights.shape[3]
    freq_block = freq_total // trace_count
    half_rank = rank_total // sub_count
    dft_rows = spectral_table(freq_total, samples)
    spectra = jnp.einsum(
        "kt,xts->xks", dft_rows, seismic, preferred_element_type=jnp.float32
    ).astype(jnp.bfloat16)
    spectra = spectra.reshape(traces_here, 2, freq_total, shots_count)
    freq_index = jnp.arange(freq_total, dtype=jnp.int32)
    band_mask = (
        (freq_index[:, None] >= band_low[None, :]) & (freq_index[:, None] < band_high[None, :])
    ).astype(jnp.bfloat16)
    masked = spectra * band_mask
    piece = masked.astype(jnp.float32)
    piece = piece.reshape(traces_here, 2, 1 * lax.axis_size("trace"), freq_block, shots_count)
    leaf_piece = leaf_weights.astype(jnp.float32)
    leaf_piece = leaf_piece.reshape(
        traces_here, 1 * lax.axis_size("trace"), freq_block, 2, rank_total
    )
    parts = jnp.einsum("iagfs,igfbr->gabrs", piece, leaf_piece, precision=highest)
    leaf_terms = lax.psum_scatter(join_complex(parts), "trace", scatter_dimension=0, tiled=True)[0]
    weights_now = lax.psum_scatter(leaf_terms, "sub", scatter_dimension=1, tiled=True)
    box_index = trace_place * space_count + space_place
    section_no = 0
    for bit_no in range(space_count.bit_length() - 1):
        partner = swap_space(weights_now, bit_no)
        weights_now = merge_level(
            weights_now,
            partner,
            section_no,
            box_index,
            translations,
            level_table,
            sub_place,
            half_rank,
        )
        section_no = section_no + 1
    for bit_no in range(trace_count.bit_length() - 1):
        partner = swap_trace(weights_now, bit_no)
        weights_now = merge_level(
            weights_now,
            partner,
            section_no,
            box_index,
            translations,
            level_table,
            sub_place,
            half_rank,
        )
        section_no = section_no + 1
    return weights_now[None]


def table_rows(freq_total, samples, chunks):
    phase = np.arange(freq_total)[:, None] * np.arange(samples)[None, :] % samples
    angle = phase.astype(np.float32) * np.float32(2.0 * math.pi / samples)
    factor = np.float32(1.0 / math.sqrt(samples))
    parts = np.stack([np.cos(angle), -np.sin(angle)]) * factor
    rows = parts.reshape(2, chunks, freq_total // chunks, samples).transpose(1, 0, 2, 3)
    return rows.reshape(chunks, 2 * freq_total // chunks, samples).astype(ml_dtypes.bfloat16)


def split_two(x):
    high = x.astype(jnp.bfloat16).astype(jnp.float32)
    return high, x - high


def fused_kernel(
    sizes,
    x_hbm,
    low_hbm,
    high_hbm,
    q_hbm,
    tab_hbm,
    tr_hbm,
    level_hbm,
    out_ref,
    band_v,
    level_ref,
    x_v,
    q_v,
    tab_v,
    tr_v,
    spec_v,
    mat_hi,
    mat_lo,
    own,
    give,
    near,
    send,
    recv,
    load_sem,
    small_sem,
    near_send_sem,
    near_recv_sem,
    send_sem,
    recv_sem,
):
    trace_count, space_count, sub_count = sizes
    t, p, u = lax.axis_index("trace"), lax.axis_index("space"), lax.axis_index("sub")
    chunks = tab_v.shape[0]
    traces = q_v.shape[0]
    pairs = traces // 2
    bands = trace_count // chunks
    boxes = trace_count * space_count
    levels = mat_hi.shape[0]
    rank = tr_v.shape[2]
    half = rank // sub_count

    band_loads = [
        pltpu.make_async_copy(low_hbm, band_v.at[0], small_sem.at[0]),
        pltpu.make_async_copy(high_hbm, band_v.at[1], small_sem.at[1]),
    ]
    level_load = pltpu.make_async_copy(level_hbm, level_ref, small_sem.at[2])
    slabs = 4
    slab = tab_v.shape[1] // slabs
    tab_loads = []
    for h in range(chunks):
        for n in range(slabs):
            rows = pl.ds(n * slab, slab)
            tab_loads.append(
                pltpu.make_async_copy(
                    tab_hbm.at[h, rows], tab_v.at[h, rows], load_sem.at[len(tab_loads)]
                )
            )
    x_loads = []
    for j in range(traces):
        x_loads.append(
            pltpu.make_async_copy(
                x_hbm.at[j],
                x_v.at[j // 2, :, pl.ds(j % 2 * LANES, LANES)],
                load_sem.at[chunks * slabs + j],
            )
        )
    q_load = pltpu.make_async_copy(q_hbm, q_v, load_sem.at[chunks * slabs + traces])
    tr_load = pltpu.make_async_copy(tr_hbm, tr_v, load_sem.at[chunks * slabs + traces + 1])
    for load in band_loads + x_loads[:2] + tab_loads[:slabs] + x_loads[2:] + tab_loads[slabs:]:
        load.start()
    tr_load.start()
    level_load.start()
    q_load.start()

    offsets = [
        (dt, dp) for dt in range(trace_count) for dp in range(space_count) if dt or dp
    ]
    offsets.sort(key=lambda o: -min(o[0], trace_count - o[0]) * 2 - o[1])

    def place(offset):
        return lax.rem(t + offset[0], trace_count), lax.rem(p + offset[1], space_count)

    sibling = {"sub": 1 - u}
    barrier = pltpu.get_barrier_semaphore()
    pl.semaphore_signal(
        barrier, inc=1, device_id=sibling, device_id_type=pl.DeviceIdType.MESH
    )
    for offset in offsets:
        tt, pp = place(offset)
        pl.semaphore_signal(
            barrier,
            inc=1,
            device_id={"trace": tt, "space": pp},
            device_id_type=pl.DeviceIdType.MESH,
        )

    def place_matrices(level, q):
        stride = 2**level
        lower = [b for b in range(boxes) if b // stride % 2 == 0][q]
        for side in range(2):
            for child in range(2 if level else 1):
                entry = level_ref[level, child if level else p, lower + side * stride]
                real, imag = tr_v[entry, 0], tr_v[entry, 1]
                columns = slice(child * LANES, (child + 1) * LANES)
                top = jnp.concatenate([real, -imag], axis=1)
                bottom = jnp.concatenate([imag, real], axis=1)
                for part, rows in enumerate((top, bottom)):
                    high, rest = split_two(rows)
                    at = (side * 2 + part) * rank
                    mat_hi[level, q, at : at + rank, columns] = high.astype(jnp.bfloat16)
                    mat_lo[level, q, at : at + rank, columns] = rest.astype(jnp.bfloat16)

    to_place = [(level, q) for level in range(levels) for q in range(boxes // 2)]
    late = pairs // 2
    per_pair = -(-len(to_place) // late)

    leaves = []
    for h in range(chunks):
        for load in tab_loads[h * slabs : (h + 1) * slabs]:
            load.wait()
        width = bands * LANES
        freq = lax.broadcasted_iota(jnp.int32, (width, LANES), 0) + h * width
        if h == 0:
            for load in band_loads:
                load.wait()
        keep = (freq >= band_v[0]) & (freq < band_v[1])
        for pair in range(pairs):
            if h == 0:
                x_loads[2 * pair].wait()
                x_loads[2 * pair + 1].wait()
            if h == chunks - 1 and pair >= pairs - late:
                if pair == pairs - late:
                    level_load.wait()
                    tr_load.wait()
                done = (pair - pairs + late) * per_pair
                for level, q in to_place[done : done + per_pair]:
                    place_matrices(level, q)
            rows = jnp.dot(tab_v[h], x_v[pair], preferred_element_type=jnp.float32)
            for part in range(2):
                for k in range(2):
                    piece = rows[part * width : (part + 1) * width, k * LANES : (k + 1) * LANES]
                    piece = jnp.where(keep, piece, 0.0).astype(jnp.bfloat16)
                    j = 2 * pair + k
                    for g in range(bands):
                        spec_v[
                            h * bands + g,
                            j * LANES : (j + 1) * LANES,
                            part * LANES : (part + 1) * LANES,
                        ] = piece[g * LANES : (g + 1) * LANES]
    q_load.wait()
    for g in range(trace_count):
        left = jnp.concatenate(
            [q_v[j, :, g * LANES : (g + 1) * LANES] for j in range(traces)], axis=1
        )
        both = jnp.dot(left, spec_v[g], preferred_element_type=jnp.float32)
        real = both[:rank, :LANES] - both[rank:, LANES:]
        imag = both[rank:, :LANES] + both[:rank, LANES:]
        leaves.append(jnp.concatenate([real, imag], axis=0))

    def apply(level, q, packed):
        depth = packed.shape[0]
        main = jnp.dot(mat_hi[level, q, :, :depth], packed, preferred_element_type=jnp.float32)
        rest = jnp.dot(
            mat_lo[level, q, :, :depth], packed[:, :LANES], preferred_element_type=jnp.float32
        )
        return main[:, :LANES] + (main[:, LANES:] + rest)

    def packed_two(value):
        return jnp.concatenate(split_two(value), axis=1).astype(jnp.bfloat16)

    def near_copy(box):
        return pltpu.make_async_remote_copy(
            src_ref=give.at[box],
            dst_ref=near.at[box],
            send_sem=near_send_sem.at[box],
            recv_sem=near_recv_sem.at[box],
            device_id=sibling,
            device_id_type=pl.DeviceIdType.MESH,
        )

    now = [None] * boxes
    for level in range(levels):
        if level == levels - 1:
            pl.semaphore_wait(barrier, len(offsets) + 1)
        stride = 2**level
        lowers = [b for b in range(boxes) if b // stride % 2 == 0]
        before = now[:]
        for q, lower in enumerate(lowers):
            if level == 0:
                packed = packed_two(leaves[q])
            else:
                packed = jnp.concatenate([before[lower], before[lower + stride]], axis=0)
            both = apply(level, q, packed)
            for side in range(2):
                mine = both[side * LANES : (side + 1) * LANES]
                box = lower + side * stride
                if level < levels - 1:
                    now[box] = packed_two(mine)
                else:
                    for part in range(2):
                        first, second = (
                            mine[part * rank + s * half : part * rank + (s + 1) * half]
                            for s in range(2)
                        )
                        rows = slice(part * half, (part + 1) * half)
                        own[box, rows] = jnp.where(u == 0, first, second)
                        give[box, rows] = jnp.where(u == 0, second, first).astype(jnp.bfloat16)
                    near_copy(box).start()

    def summed(box):
        near_copy(box).wait_recv()
        return own[box] + near[box].astype(jnp.float32)

    copies = []
    for i, offset in enumerate(offsets):
        tt, pp = place(offset)
        send[i] = summed(tt * space_count + pp).astype(jnp.bfloat16)
        copy = pltpu.make_async_remote_copy(
            src_ref=send.at[i],
            dst_ref=recv.at[i],
            send_sem=send_sem.at[i],
            recv_sem=recv_sem.at[i],
            device_id={"trace": tt, "space": pp},
            device_id_type=pl.DeviceIdType.MESH,
        )
        copy.start()
        copies.append(copy)
    total = summed(t * space_count + p)
    for i in reversed(range(len(offsets))):
        copies[i].wait_recv()
        total = total + recv[i].astype(jnp.float32)
    out_ref[...] = total.reshape(1, 2, half, LANES)
    for box in range(boxes):
        near_copy(box).wait_send()
    for copy in copies:
        copy.wait_send()


def fused_device(seismic, band_low, band_high, leaf_weights, translations, level_table):
    sizes = tuple(lax.axis_size(name) for name in ("trace", "space", "sub"))
    boxes = sizes[0] * sizes[1]
    traces, samples, shots = seismic.shape
    freq_total, rank = leaf_weights.shape[1], leaf_weights.shape[3]
    chunks = 2
    levels = level_table.shape[0]
    table = jnp.asarray(table_rows(freq_total, samples, chunks))
    weights = leaf_weights.transpose(0, 2, 3, 1).reshape(traces, 2 * rank, freq_total)
    half = rank // sizes[2]
    hbm_spec = pl.BlockSpec(memory_space=pltpu.HBM)
    vmem_spec = pl.BlockSpec(memory_space=pltpu.VMEM)
    dma = pltpu.SemaphoreType.DMA
    return pl.pallas_call(
        functools.partial(fused_kernel, sizes),
        out_shape=jax.ShapeDtypeStruct((1, 2, rank // sizes[2], shots), jnp.float32),
        in_specs=[hbm_spec] * 7,
        out_specs=vmem_spec,
        scratch_shapes=[
            pltpu.VMEM((2, 1, shots), jnp.int32),
            pltpu.SMEM((levels, 2, boxes), jnp.int32),
            pltpu.VMEM((traces // 2, samples, 2 * shots), jnp.bfloat16),
            pltpu.VMEM(weights.shape, jnp.bfloat16),
            pltpu.VMEM(table.shape, jnp.bfloat16),
            pltpu.VMEM(translations.shape, jnp.float32),
            pltpu.VMEM((sizes[0], traces * LANES, 2 * LANES), jnp.bfloat16),
            pltpu.VMEM((levels, boxes // 2, 4 * rank, 4 * rank), jnp.bfloat16),
            pltpu.VMEM((levels, boxes // 2, 4 * rank, 4 * rank), jnp.bfloat16),
            pltpu.VMEM((boxes, 2 * half, shots), jnp.float32),
            pltpu.VMEM((boxes, 2 * half, shots), jnp.bfloat16),
            pltpu.VMEM((boxes, 2 * half, shots), jnp.bfloat16),
            pltpu.VMEM((boxes - 1, 2 * half, shots), jnp.bfloat16),
            pltpu.VMEM((boxes - 1, 2 * half, shots), jnp.bfloat16),
            dma((4 * chunks + traces + 2,)),
            dma((3,)),
            dma((boxes,)),
            dma((boxes,)),
            dma((boxes - 1,)),
            dma((boxes - 1,)),
        ],
        compiler_params=pltpu.CompilerParams(
            collective_id=0, has_side_effects=True, vmem_limit_bytes=56 * 2**20
        ),
    )(
        seismic,
        band_low.reshape(1, shots),
        band_high.reshape(1, shots),
        weights,
        table,
        translations,
        level_table.transpose(0, 2, 1),
    )


def per_device(seismic, band_low, band_high, leaf_weights, translations, level_table):
    trace_count, space_count, sub_count = (
        lax.axis_size(name) for name in ("trace", "space", "sub")
    )
    traces, _, shots = seismic.shape
    freq_total, rank = leaf_weights.shape[1], leaf_weights.shape[3]
    fits = (
        shots == LANES
        and freq_total == trace_count * LANES
        and 2 * rank == LANES
        and space_count == 2
        and sub_count == 2
        and traces % 2 == 0
        and trace_count % 2 == 0
    )
    chosen = fused_device if fits else general_device
    return chosen(seismic, band_low, band_high, leaf_weights, translations, level_table)


def solution(mesh):
    placed = (
        P(("groups", "trace", "space", "sub"), None, None),
        P("groups"),
        P("groups"),
        P(),
        P(),
        P(),
    )
    return jax.shard_map(
        per_device,
        mesh=mesh,
        in_specs=placed,
        out_specs=P(("groups", "trace", "space"), None, "sub", None),
        check_vma=False,
    )
```

```python
import functools
import math

import jax
import jax.numpy as jnp
import ml_dtypes
import numpy as np
from jax import lax
from jax.experimental import pallas as pl
from jax.experimental.pallas import tpu as pltpu
from jax.sharding import PartitionSpec as P

LANES = 128


def swapped(x, axis, distance):
    return lax.ppermute(x, axis, [(i, i ^ 1 << distance) for i in range(lax.axis_size(axis))])


def spectral_table(freq_total, samples):
    freq_range = jnp.arange(freq_total, dtype=jnp.int32)
    time_range = jnp.arange(samples, dtype=jnp.int32)
    phase = freq_range[:, None] * time_range[None, :] % samples
    angle = phase.astype(jnp.float32) * (2.0 * math.pi / samples)
    factor = 1.0 / math.sqrt(samples)
    return (jnp.concatenate([jnp.cos(angle), -jnp.sin(angle)], axis=0) * factor).astype(
        jnp.bfloat16
    )


def complex_product(left, right):
    highest = lax.Precision.HIGHEST
    real_part = jnp.dot(left[0], right[0], precision=highest) - jnp.dot(
        left[1], right[1], precision=highest
    )
    imag_part = jnp.dot(left[0], right[1], precision=highest) + jnp.dot(
        left[1], right[0], precision=highest
    )
    return jnp.stack([real_part, imag_part])


def swap_space(weights_now, bit_no):
    return swapped(weights_now, "space", bit_no)


def swap_trace(weights_now, bit_no):
    return swapped(weights_now, "trace", bit_no)


def merge_level(
    weights_now, partner, section_no, box_index, translations, level_table, sub_place, half_rank
):
    stride = 2**section_no
    upper_flag = box_index // stride % 2 == 1
    lower_part = jnp.where(upper_flag, partner, weights_now)
    upper_part = jnp.where(upper_flag, weights_now, partner)
    entries = lax.dynamic_index_in_dim(level_table[section_no], box_index, 0, keepdims=False)
    first_mat = lax.dynamic_index_in_dim(translations, entries[0], 0, keepdims=False)
    second_mat = lax.dynamic_index_in_dim(translations, entries[1], 0, keepdims=False)
    full_lower, full_upper = (
        lax.all_gather(lower_part, "sub", axis=1, tiled=True),
        lax.all_gather(upper_part, "sub", axis=1, tiled=True),
    )
    first_rows = lax.dynamic_slice_in_dim(first_mat, sub_place * half_rank, half_rank, 1)
    second_rows = lax.dynamic_slice_in_dim(second_mat, sub_place * half_rank, half_rank, 1)
    return complex_product(first_rows, full_lower) + complex_product(second_rows, full_upper)


def join_complex(parts):
    return jnp.stack([parts[:, 0, 0] - parts[:, 1, 1], parts[:, 0, 1] + parts[:, 1, 0]], axis=1)


def general_device(seismic, band_low, band_high, leaf_weights, translations, level_table):
    highest = lax.Precision.HIGHEST
    trace_count = lax.axis_size("trace")
    space_count = lax.axis_size("space")
    sub_count = lax.axis_size("sub")
    trace_place = lax.axis_index("trace")
    space_place = lax.axis_index("space")
    sub_place = lax.axis_index("sub")
    traces_here = seismic.shape[0]
    samples = seismic.shape[1]
    shots_count = seismic.shape[2]
    freq_total = leaf_weights.shape[1]
    rank_total = leaf_weights.shape[3]
    freq_block = freq_total // trace_count
    half_rank = rank_total // sub_count
    dft_rows = spectral_table(freq_total, samples)
    spectra = jnp.einsum(
        "kt,xts->xks", dft_rows, seismic, preferred_element_type=jnp.float32
    ).astype(jnp.bfloat16)
    spectra = spectra.reshape(traces_here, 2, freq_total, shots_count)
    freq_index = jnp.arange(freq_total, dtype=jnp.int32)
    band_mask = (
        (freq_index[:, None] >= band_low[None, :]) & (freq_index[:, None] < band_high[None, :])
    ).astype(jnp.bfloat16)
    masked = spectra * band_mask
    piece = masked.astype(jnp.float32)
    piece = piece.reshape(traces_here, 2, 1 * lax.axis_size("trace"), freq_block, shots_count)
    leaf_piece = leaf_weights.astype(jnp.float32)
    leaf_piece = leaf_piece.reshape(
        traces_here, 1 * lax.axis_size("trace"), freq_block, 2, rank_total
    )
    parts = jnp.einsum("iagfs,igfbr->gabrs", piece, leaf_piece, precision=highest)
    leaf_terms = lax.psum_scatter(join_complex(parts), "trace", scatter_dimension=0, tiled=True)[0]
    weights_now = lax.psum_scatter(leaf_terms, "sub", scatter_dimension=1, tiled=True)
    box_index = trace_place * space_count + space_place
    section_no = 0
    for bit_no in range(space_count.bit_length() - 1):
        partner = swap_space(weights_now, bit_no)
        weights_now = merge_level(
            weights_now,
            partner,
            section_no,
            box_index,
            translations,
            level_table,
            sub_place,
            half_rank,
        )
        section_no = section_no + 1
    for bit_no in range(trace_count.bit_length() - 1):
        partner = swap_trace(weights_now, bit_no)
        weights_now = merge_level(
            weights_now,
            partner,
            section_no,
            box_index,
            translations,
            level_table,
            sub_place,
            half_rank,
        )
        section_no = section_no + 1
    return weights_now[None]


def table_rows(freq_total, samples, chunks):
    phase = np.arange(freq_total)[:, None] * np.arange(samples)[None, :] % samples
    angle = phase.astype(np.float32) * np.float32(2.0 * math.pi / samples)
    factor = np.float32(1.0 / math.sqrt(samples))
    parts = np.stack([np.cos(angle), -np.sin(angle)]) * factor
    rows = parts.reshape(2, chunks, freq_total // chunks, samples).transpose(1, 0, 2, 3)
    return rows.reshape(chunks, 2 * freq_total // chunks, samples).astype(ml_dtypes.bfloat16)


def split_two(x):
    high = x.astype(jnp.bfloat16).astype(jnp.float32)
    return high, x - high


def fused_kernel(
    sizes,
    x_hbm,
    low_hbm,
    high_hbm,
    q_hbm,
    tab_hbm,
    tr_hbm,
    level_hbm,
    out_ref,
    band_v,
    level_ref,
    x_v,
    q_v,
    tab_v,
    tr_v,
    spec_v,
    mat_hi,
    mat_lo,
    own,
    give,
    near,
    send,
    recv,
    load_sem,
    small_sem,
    near_send_sem,
    near_recv_sem,
    send_sem,
    recv_sem,
):
    trace_count, space_count, sub_count = sizes
    t, p, u = lax.axis_index("trace"), lax.axis_index("space"), lax.axis_index("sub")
    chunks = tab_v.shape[0]
    traces = q_v.shape[0]
    pairs = traces // 2
    bands = trace_count // chunks
    boxes = trace_count * space_count
    levels = mat_hi.shape[0]
    rank = tr_v.shape[2]
    half = rank // sub_count

    band_loads = [
        pltpu.make_async_copy(low_hbm, band_v.at[0], small_sem.at[0]),
        pltpu.make_async_copy(high_hbm, band_v.at[1], small_sem.at[1]),
    ]
    level_load = pltpu.make_async_copy(level_hbm, level_ref, small_sem.at[2])
    slabs = 4
    slab = tab_v.shape[1] // slabs
    tab_loads = []
    for h in range(chunks):
        for n in range(slabs):
            rows = pl.ds(n * slab, slab)
            tab_loads.append(
                pltpu.make_async_copy(
                    tab_hbm.at[h, rows], tab_v.at[h, rows], load_sem.at[len(tab_loads)]
                )
            )
    x_loads = []
    for j in range(traces):
        x_loads.append(
            pltpu.make_async_copy(
                x_hbm.at[j],
                x_v.at[j // 2, :, pl.ds(j % 2 * LANES, LANES)],
                load_sem.at[chunks * slabs + j],
            )
        )
    q_load = pltpu.make_async_copy(q_hbm, q_v, load_sem.at[chunks * slabs + traces])
    tr_load = pltpu.make_async_copy(tr_hbm, tr_v, load_sem.at[chunks * slabs + traces + 1])
    for load in band_loads + x_loads[:2] + tab_loads[:slabs] + x_loads[2:] + tab_loads[slabs:]:
        load.start()
    tr_load.start()
    level_load.start()
    q_load.start()

    offsets = [
        (dt, dp) for dt in range(trace_count) for dp in range(space_count) if dt or dp
    ]
    offsets.sort(key=lambda o: -min(o[0], trace_count - o[0]) * 2 - o[1])

    def place(offset):
        return lax.rem(t + offset[0], trace_count), lax.rem(p + offset[1], space_count)

    sibling = {"sub": 1 - u}
    barrier = pltpu.get_barrier_semaphore()
    pl.semaphore_signal(
        barrier, inc=1, device_id=sibling, device_id_type=pl.DeviceIdType.MESH
    )
    for offset in offsets:
        tt, pp = place(offset)
        pl.semaphore_signal(
            barrier,
            inc=1,
            device_id={"trace": tt, "space": pp},
            device_id_type=pl.DeviceIdType.MESH,
        )

    def place_matrices(level, q):
        stride = 2**level
        lower = [b for b in range(boxes) if b // stride % 2 == 0][q]
        for side in range(2):
            for child in range(2 if level else 1):
                entry = level_ref[level, child if level else p, lower + side * stride]
                real, imag = tr_v[entry, 0], tr_v[entry, 1]
                columns = slice(child * LANES, (child + 1) * LANES)
                top = jnp.concatenate([real, -imag], axis=1)
                bottom = jnp.concatenate([imag, real], axis=1)
                for part, rows in enumerate((top, bottom)):
                    high, rest = split_two(rows)
                    at = (side * 2 + part) * rank
                    mat_hi[level, q, at : at + rank, columns] = high.astype(jnp.bfloat16)
                    mat_lo[level, q, at : at + rank, columns] = rest.astype(jnp.bfloat16)

    to_place = [(level, q) for level in range(levels) for q in range(boxes // 2)]
    late = pairs // 2
    per_pair = -(-len(to_place) // late)

    leaves = []
    for h in range(chunks):
        for load in tab_loads[h * slabs : (h + 1) * slabs]:
            load.wait()
        width = bands * LANES
        freq = lax.broadcasted_iota(jnp.int32, (width, LANES), 0) + h * width
        if h == 0:
            for load in band_loads:
                load.wait()
        keep = (freq >= band_v[0]) & (freq < band_v[1])
        for pair in range(pairs):
            if h == 0:
                x_loads[2 * pair].wait()
                x_loads[2 * pair + 1].wait()
            if h == chunks - 1 and pair >= pairs - late:
                if pair == pairs - late:
                    level_load.wait()
                    tr_load.wait()
                done = (pair - pairs + late) * per_pair
                for level, q in to_place[done : done + per_pair]:
                    place_matrices(level, q)
            for part in range(2):
                rows = jnp.dot(
                    tab_v[h, part * width : (part + 1) * width],
                    x_v[pair],
                    preferred_element_type=jnp.float32,
                )
                for k in range(2):
                    piece = rows[:, k * LANES : (k + 1) * LANES]
                    piece = jnp.where(keep, piece, 0.0).astype(jnp.bfloat16)
                    j = 2 * pair + k
                    for g in range(bands):
                        spec_v[
                            h * bands + g,
                            j * LANES : (j + 1) * LANES,
                            part * LANES : (part + 1) * LANES,
                        ] = piece[g * LANES : (g + 1) * LANES]
    q_load.wait()
    for g in range(trace_count):
        left = jnp.concatenate(
            [q_v[j, :, g * LANES : (g + 1) * LANES] for j in range(traces)], axis=1
        )
        both = jnp.dot(left, spec_v[g], preferred_element_type=jnp.float32)
        real = both[:rank, :LANES] - both[rank:, LANES:]
        imag = both[rank:, :LANES] + both[:rank, LANES:]
        leaves.append(jnp.concatenate([real, imag], axis=0))

    def apply(level, q, packed):
        depth = packed.shape[0]
        main = jnp.dot(mat_hi[level, q, :, :depth], packed, preferred_element_type=jnp.float32)
        rest = jnp.dot(
            mat_lo[level, q, :, :depth], packed[:, :LANES], preferred_element_type=jnp.float32
        )
        return main[:, :LANES] + (main[:, LANES:] + rest)

    def packed_two(value):
        return jnp.concatenate(split_two(value), axis=1).astype(jnp.bfloat16)

    def near_copy(box):
        return pltpu.make_async_remote_copy(
            src_ref=give.at[box],
            dst_ref=near.at[box],
            send_sem=near_send_sem.at[box],
            recv_sem=near_recv_sem.at[box],
            device_id=sibling,
            device_id_type=pl.DeviceIdType.MESH,
        )

    now = [None] * boxes
    for level in range(levels):
        if level == levels - 1:
            pl.semaphore_wait(barrier, len(offsets) + 1)
        stride = 2**level
        lowers = [b for b in range(boxes) if b // stride % 2 == 0]
        before = now[:]
        for q, lower in enumerate(lowers):
            if level == 0:
                packed = packed_two(leaves[q])
            else:
                packed = jnp.concatenate([before[lower], before[lower + stride]], axis=0)
            both = apply(level, q, packed)
            for side in range(2):
                mine = both[side * LANES : (side + 1) * LANES]
                box = lower + side * stride
                if level < levels - 1:
                    now[box] = packed_two(mine)
                else:
                    for part in range(2):
                        first, second = (
                            mine[part * rank + s * half : part * rank + (s + 1) * half]
                            for s in range(2)
                        )
                        rows = slice(part * half, (part + 1) * half)
                        own[box, rows] = jnp.where(u == 0, first, second)
                        give[box, rows] = jnp.where(u == 0, second, first).astype(jnp.bfloat16)
                    near_copy(box).start()

    def summed(box):
        near_copy(box).wait_recv()
        return own[box] + near[box].astype(jnp.float32)

    copies = []
    for i, offset in enumerate(offsets):
        tt, pp = place(offset)
        send[i] = summed(tt * space_count + pp).astype(jnp.bfloat16)
        copy = pltpu.make_async_remote_copy(
            src_ref=send.at[i],
            dst_ref=recv.at[i],
            send_sem=send_sem.at[i],
            recv_sem=recv_sem.at[i],
            device_id={"trace": tt, "space": pp},
            device_id_type=pl.DeviceIdType.MESH,
        )
        copy.start()
        copies.append(copy)
    total = summed(t * space_count + p)
    for i in reversed(range(len(offsets))):
        copies[i].wait_recv()
        total = total + recv[i].astype(jnp.float32)
    out_ref[...] = total.reshape(1, 2, half, LANES)
    for box in range(boxes):
        near_copy(box).wait_send()
    for copy in copies:
        copy.wait_send()


def fused_device(seismic, band_low, band_high, leaf_weights, translations, level_table):
    sizes = tuple(lax.axis_size(name) for name in ("trace", "space", "sub"))
    boxes = sizes[0] * sizes[1]
    traces, samples, shots = seismic.shape
    freq_total, rank = leaf_weights.shape[1], leaf_weights.shape[3]
    chunks = 2
    levels = level_table.shape[0]
    table = jnp.asarray(table_rows(freq_total, samples, chunks))
    weights = leaf_weights.transpose(0, 2, 3, 1).reshape(traces, 2 * rank, freq_total)
    half = rank // sizes[2]
    hbm_spec = pl.BlockSpec(memory_space=pltpu.HBM)
    vmem_spec = pl.BlockSpec(memory_space=pltpu.VMEM)
    dma = pltpu.SemaphoreType.DMA
    return pl.pallas_call(
        functools.partial(fused_kernel, sizes),
        out_shape=jax.ShapeDtypeStruct((1, 2, rank // sizes[2], shots), jnp.float32),
        in_specs=[hbm_spec] * 7,
        out_specs=vmem_spec,
        scratch_shapes=[
            pltpu.VMEM((2, 1, shots), jnp.int32),
            pltpu.SMEM((levels, 2, boxes), jnp.int32),
            pltpu.VMEM((traces // 2, samples, 2 * shots), jnp.bfloat16),
            pltpu.VMEM(weights.shape, jnp.bfloat16),
            pltpu.VMEM(table.shape, jnp.bfloat16),
            pltpu.VMEM(translations.shape, jnp.float32),
            pltpu.VMEM((sizes[0], traces * LANES, 2 * LANES), jnp.bfloat16),
            pltpu.VMEM((levels, boxes // 2, 4 * rank, 4 * rank), jnp.bfloat16),
            pltpu.VMEM((levels, boxes // 2, 4 * rank, 4 * rank), jnp.bfloat16),
            pltpu.VMEM((boxes, 2 * half, shots), jnp.float32),
            pltpu.VMEM((boxes, 2 * half, shots), jnp.bfloat16),
            pltpu.VMEM((boxes, 2 * half, shots), jnp.bfloat16),
            pltpu.VMEM((boxes - 1, 2 * half, shots), jnp.bfloat16),
            pltpu.VMEM((boxes - 1, 2 * half, shots), jnp.bfloat16),
            dma((4 * chunks + traces + 2,)),
            dma((3,)),
            dma((boxes,)),
            dma((boxes,)),
            dma((boxes - 1,)),
            dma((boxes - 1,)),
        ],
        compiler_params=pltpu.CompilerParams(
            collective_id=0, has_side_effects=True, vmem_limit_bytes=56 * 2**20
        ),
    )(
        seismic,
        band_low.reshape(1, shots),
        band_high.reshape(1, shots),
        weights,
        table,
        translations,
        level_table.transpose(0, 2, 1),
    )


def per_device(seismic, band_low, band_high, leaf_weights, translations, level_table):
    trace_count, space_count, sub_count = (
        lax.axis_size(name) for name in ("trace", "space", "sub")
    )
    traces, _, shots = seismic.shape
    freq_total, rank = leaf_weights.shape[1], leaf_weights.shape[3]
    fits = (
        shots == LANES
        and freq_total == trace_count * LANES
        and 2 * rank == LANES
        and space_count == 2
        and sub_count == 2
        and traces % 2 == 0
        and trace_count % 2 == 0
    )
    chosen = fused_device if fits else general_device
    return chosen(seismic, band_low, band_high, leaf_weights, translations, level_table)


def solution(mesh):
    placed = (
        P(("groups", "trace", "space", "sub"), None, None),
        P("groups"),
        P("groups"),
        P(),
        P(),
        P(),
    )
    return jax.shard_map(
        per_device,
        mesh=mesh,
        in_specs=placed,
        out_specs=P(("groups", "trace", "space"), None, "sub", None),
        check_vma=False,
    )
```
